512 devices in a mesh: gx: 32 (over y, x), gy: 16 (over z, core).
Axes of the slice: x: 4, y: 8, z: 8, core: 2. Of those that a mesh axis runs over, the one named last changes fastest.
Arguments:
- panel: bfloat16 [32, 16, 2, 128, 1024], P('gx', 'gy'), may hold values from -0.5 to 0.5
- corner_panel: bfloat16 [32, 16, 2, 24, 128], P('gx', 'gy'), may hold values from -0.5 to 0.5
- interface_diag: float32 [32, 16, 2, 1024], P('gx', 'gy'), may hold values from 0.5 to 2
- coarse_diag: float32 [32, 512], P('gx'), may hold values from 0.5 to 2
- scaling: float32 [32, 16, 8, 128], P('gx', 'gy'), may hold values from 0.5 to 2
- dual_rhs: float32 [32, 16, 8, 128], P('gx', 'gy'), may hold values from -6 to 6
- block_map: int32 [32, 16, 2, 8], P('gx', 'gy'), may hold values from 0 to 39
- corner_map: int32 [32, 16, 2, 24], P('gx', 'gy'), may hold values from 0 to 511
- counts: int32 [32, 16], P('gx', 'gy'), may hold values from 1 to 2, as said below
Outputs:
- multipliers: float32 [32, 16, 8, 128], P('gx', 'gy')
- residual: float32 [32, 16, 8, 128], P('gx', 'gy')
The draws below stay inside these ranges and needn't reach their ends.
Inputs may be any that keep to these rules, and one draw needn't show every extreme that they name: `counts`: every device holds one or more live subdomains in its first slots; some device has all 2 slots live and some has one.
All inputs are finite; a program needn't handle non-finite values.
Results may differ from the reference program's by a relative error of at most 0.0003.
Values sent between devices are 32-bit elements; how exact they have to be, the bound alone decides.
No kernel may reach another device: no remote copies, remote signals or barrier semaphores. Data moves between devices by JAX's collectives and lax.ppermute only.
A program may use at most 64 MiB of HBM per device.

```python
import math
import jax
import jax.numpy as jnp
from jax import lax

NI = 1024
BLK = 128
NBLK = 8
NP = 128
SD_DEV = 2
MB_DEV = 8
NCOR = 24
NCO = 512
ITERS = 3
SUB_X = 32
SUB_Y = 16


def draw_counts(key, part):
    values = jax.random.randint(key, (SUB_X, SUB_Y), 1, SD_DEV + 1)
    values = values.at[0, 0].set(SD_DEV)
    values = values.at[SUB_X - 1, SUB_Y - 1].set(1)
    return values.astype(jnp.int32)


def with_ends(values, own_key, least, top_value):
    dims = values.shape
    spot = [jax.random.randint(jax.random.fold_in(own_key, axis), (), 0, dims[axis]) for axis in range(len(dims))]
    values = values.at[tuple(spot)].set(least)
    longest = dims.index(max(dims))
    spot[longest] = (spot[longest] + 1) % dims[longest]
    return values.at[tuple(spot)].set(top_value)


def steps_of(rng, dims, cuts, least, largest):
    level, own = 1.0, jax.random.fold_in(rng, 6)
    for axis_at, shards_of in cuts:
        steps = jnp.exp(jax.random.uniform(jax.random.fold_in(own, axis_at), (shards_of,), jnp.float32, least / len(cuts), largest / len(cuts)))
        level = level * jnp.repeat(steps, dims[axis_at] // shards_of).reshape([-1 if axis == axis_at else 1 for axis in range(len(dims))])
    return level


def centred(own_key, shape, width, reach, cuts=(), held_as=jnp.bfloat16):
    level = steps_of(own_key, shape, cuts, -0.22, 0.18) if cuts else 1.0
    entries = jax.random.normal(own_key, shape, jnp.float32) * width * level
    return jnp.minimum(jnp.maximum(entries, -reach), reach).astype(held_as)


def setup_inputs(seed: int = 0) -> dict:
    seeds = jax.random.split(jax.random.key(seed), 10)
    return {
        "panel": centred(seeds[0], (SUB_X, SUB_Y, SD_DEV, NP, NI), NP ** -0.5, 0.5, ((0, 32), (1, 16))),
        "corner_panel": centred(seeds[1], (SUB_X, SUB_Y, SD_DEV, NCOR, NP), NP ** -0.5, 0.5, ((0, 32), (1, 16))),
        "interface_diag": jnp.clip(jnp.exp(math.log(2.0) - 1.3862944 * jax.random.uniform(seeds[2], (SUB_X, SUB_Y, SD_DEV, NI), jnp.float32) ** steps_of(seeds[2], (SUB_X, SUB_Y, SD_DEV, NI), ((0, 32), (1, 16)), -0.2, 0.2)), 0.5, 2.0),
        "coarse_diag": jnp.clip(jnp.exp(math.log(2.0) - 1.3862944 * jax.random.uniform(seeds[3], (SUB_X, NCO), jnp.float32) ** steps_of(seeds[3], (SUB_X, NCO), ((0, 32),), -0.2, 0.2)), 0.5, 2.0),
        "scaling": jnp.clip(jnp.exp(math.log(2.0) - 1.3862944 * jax.random.uniform(seeds[4], (SUB_X, SUB_Y, MB_DEV, BLK), jnp.float32) ** steps_of(seeds[4], (SUB_X, SUB_Y, MB_DEV, BLK), ((0, 32), (1, 16)), -0.2, 0.2)), 0.5, 2.0),
        "dual_rhs": centred(seeds[5], (SUB_X, SUB_Y, MB_DEV, BLK), 1.0, 6.0, ((0, 32), (1, 16)), jnp.float32),
        "block_map": with_ends(jax.random.randint(seeds[6], (SUB_X, SUB_Y, SD_DEV, NBLK), 0, 5 * MB_DEV), jax.random.fold_in(seeds[6], 1), 0, (5 * MB_DEV) - 1).astype(jnp.int32),
        "corner_map": with_ends(jax.random.randint(seeds[7], (SUB_X, SUB_Y, SD_DEV, NCOR), 0, NCO), jax.random.fold_in(seeds[7], 1), 0, NCO - 1).astype(jnp.int32),
        "counts": draw_counts(jax.random.fold_in(seeds[9], 71), 0),
    }


def reference(panel, corner_panel, interface_diag, coarse_diag, scaling, dual_rhs, block_map, corner_map, counts):
    highest = lax.Precision.HIGHEST
    owned = MB_DEV
    live = (lax.iota(jnp.int32, SD_DEV)[None, None, :] < counts[:, :, None]).astype(jnp.float32)

    def corner_row(pieces):
        factor_row, corner_row_panel = pieces
        factor_wide = factor_row.astype(jnp.float32)
        corner_wide = corner_row_panel.astype(jnp.float32)
        rows_coupled = jnp.einsum('yscn,ysni->ysci', corner_wide, factor_wide, precision=highest)
        blocks_coupled = jnp.einsum('yscn,ysdn->yscd', corner_wide, corner_wide, precision=highest)
        return (rows_coupled, blocks_coupled)
    coupling, corner_block = lax.map(corner_row, (panel, corner_panel))
    corner_block = corner_block * live[:, :, :, None, None]
    corner_hot = (corner_map[..., None] == lax.iota(jnp.int32, NCO)).astype(jnp.float32)
    spread = jnp.einsum('xysco,xyscd->xysod', corner_hot, corner_block, precision=highest)
    assembled = jnp.einsum('xysod,xysdp->xop', spread, corner_hot, precision=highest)
    coarse_eye = (lax.iota(jnp.int32, NCO)[:, None] == lax.iota(jnp.int32, NCO)[None, :]).astype(jnp.float32)
    system = assembled + coarse_diag[:, :, None] * coarse_eye[None]
    factor = jnp.linalg.cholesky(system)
    signs = jnp.where(block_map < owned, 1.0, -1.0) * live[..., None]
    picker = (block_map[..., None] == lax.iota(jnp.int32, 5 * owned)).astype(jnp.float32) * signs[..., None]

    def local_row(pieces):
        factor_row, vector_row, diag_row = pieces
        factor_wide = factor_row.astype(jnp.float32)
        inner_rows = jnp.einsum('ysni,ysi->ysn', factor_wide, vector_row, precision=highest)
        return diag_row * vector_row + jnp.einsum('ysni,ysn->ysi', factor_wide, inner_rows, precision=highest)

    def solve_one(lower, right):
        return jax.scipy.linalg.cho_solve((lower, True), right)

    def operate(field):
        padded = jnp.pad(field, ((1, 1), (1, 1), (0, 0), (0, 0)))
        candidates = jnp.concatenate([field, padded[2:, 1:-1], padded[:-2, 1:-1], padded[1:-1, 2:], padded[1:-1, :-2]], axis=2)
        gathered = jnp.einsum('xysbk,xykc->xysbc', picker, candidates, precision=highest)
        gathered = gathered.reshape(SUB_X, SUB_Y, SD_DEV, NI)
        result = lax.map(local_row, (panel, gathered, interface_diag))
        corner_values = jnp.einsum('xysci,xysi->xysc', coupling, gathered, precision=highest) * live[..., None]
        coarse_right = jnp.einsum('xysco,xysc->xo', corner_hot, corner_values, precision=highest)
        coarse_sol = jax.vmap(solve_one)(factor, coarse_right)
        back_values = jnp.einsum('xysco,xo->xysc', corner_hot, coarse_sol, precision=highest)
        result = result + jnp.einsum('xysci,xysc->xysi', coupling, back_values, precision=highest)
        contrib = jnp.einsum('xysbk,xysbc->xykc', picker, result.reshape(SUB_X, SUB_Y, SD_DEV, NBLK, BLK), precision=highest)
        pads = [jnp.pad(contrib[:, :, k * owned:(k + 1) * owned], ((1, 1), (1, 1), (0, 0), (0, 0))) for k in range(1, 5)]
        image = field + contrib[:, :, :owned]
        image = image + pads[0][:-2, 1:-1] + pads[1][2:, 1:-1] + pads[2][1:-1, :-2] + pads[3][1:-1, 2:]
        return image
    multipliers = jnp.zeros_like(dual_rhs)
    residual = dual_rhs
    direction = scaling * residual
    norm_now = jnp.sum(residual * direction)
    for sweep_index in range(ITERS):
        image = operate(direction)
        alpha = norm_now / jnp.sum(direction * image)
        multipliers = multipliers + alpha * direction
        residual = dual_rhs - operate(multipliers)
        precond = scaling * residual
        norm_next = jnp.sum(residual * precond)
        direction = precond + norm_next / norm_now * direction
        norm_now = norm_next
    return (multipliers, residual)
```

```python
import functools

import jax
import jax.numpy as jnp
from jax import lax
from jax.experimental import pallas as pl
from jax.experimental.pallas import tpu as pltpu
from jax.sharding import PartitionSpec as P

F32 = jnp.float32
BF16 = jnp.bfloat16
STEP = 0.00390625
LANES = 128
PIVOTS = 4


def iota(shape, dim):
    return lax.broadcasted_iota(jnp.int32, shape, dim)


def high(a, b):
    return jnp.dot(a, b, precision=lax.Precision.HIGHEST, preferred_element_type=F32)


def thirds(x):
    first = x.astype(BF16).astype(F32)
    rest = x - first
    second = rest.astype(BF16).astype(F32)
    return first, second, rest - second


def stacked(row):
    first, second, third = thirds(row)
    at = iota((16, 1), 0)
    rows = jnp.where(at == 0, first, jnp.where(at == 1, second, jnp.where(at == 2, third, 0.0)))
    return rows.astype(BF16)


def row_times(row, matrix, dim):
    out = lax.dot_general(
        stacked(row), matrix, (((1,), (dim,)), ((), ())), preferred_element_type=F32
    )
    return jnp.sum(out[:8], axis=0, keepdims=True)


def exact_times(x, hot):
    return sum(jnp.dot(piece.astype(BF16), hot, preferred_element_type=F32) for piece in thirds(x))


def inverse2(a, b, c):
    r = 1.0 / (a * c - b * b)
    return c * r, -b * r, a * r


def pivot_inverse(e):
    p = inverse2(e(0, 0), e(0, 1), e(1, 1))
    b = [[e(0, 2), e(0, 3)], [e(1, 2), e(1, 3)]]
    u = [
        [p[0] * b[0][j] + p[1] * b[1][j] for j in (0, 1)],
        [p[1] * b[0][j] + p[2] * b[1][j] for j in (0, 1)],
    ]
    s = inverse2(
        e(2, 2) - (b[0][0] * u[0][0] + b[1][0] * u[1][0]),
        e(2, 3) - (b[0][0] * u[0][1] + b[1][0] * u[1][1]),
        e(3, 3) - (b[0][1] * u[0][1] + b[1][1] * u[1][1]),
    )
    x = [[u[i][0] * s[0] + u[i][1] * s[1], u[i][0] * s[1] + u[i][1] * s[2]] for i in (0, 1)]
    p00 = p[0] + x[0][0] * u[0][0] + x[0][1] * u[0][1]
    p01 = p[1] + x[0][0] * u[1][0] + x[0][1] * u[1][1]
    p11 = p[2] + x[1][0] * u[1][0] + x[1][1] * u[1][1]
    return [
        [p00, p01, -x[0][0], -x[0][1]],
        [p01, p11, -x[1][0], -x[1][1]],
        [-x[0][0], -x[1][0], s[0], s[1]],
        [-x[0][1], -x[1][1], s[1], s[2]],
    ]


def small_inverse(a, n):
    lane = iota((1, n), 1)
    at8 = iota((8, 1), 0)
    for k in range(0, n, PIVOTS):
        rows = [a[k + i : k + i + 1, :] for i in range(PIVOTS)]
        cols = [jnp.broadcast_to(a[:, k + i : k + i + 1], (n, n)) for i in range(PIVOTS)]
        w = pivot_inverse(lambda i, j: cols[j][k + i : k + i + 1, :])
        inside = (lane >= k) & (lane < k + PIVOTS)
        units = [
            jnp.where(inside, jnp.where(lane == k + i, 1.0, 0.0), rows[i]) for i in range(PIVOTS)
        ]
        fresh = [sum(w[i][j] * units[j] for j in range(PIVOTS)) for i in range(PIVOTS)]
        base = jnp.where(inside, 0.0, a)
        for i in range(PIVOTS):
            base = base - cols[i] * fresh[i]
        v = k // 8 * 8
        block = base[v : v + 8]
        for i in range(PIVOTS):
            block = jnp.where(at8 == k + i - v, fresh[i], block)
        a = jnp.concatenate([x for x in (base[:v], block, base[v + 8 :]) if x.shape[0]], axis=0)
    return a


def setup_kernel(
    panel_hbm, corner_hbm, diag_hbm, place_hbm, map_hbm, count_hbm, scale_hbm, rhs_hbm, v_ref,
    scale_ref, rhs_ref, pack_ref, report_ref, rows_ref, facts_ref, panel_ref, corner_ref, diag_ref,
    place_ref, map_ref, count_ref, facts, sems,
):
    slots, rows, width = panel_ref.shape
    corners = corner_ref.shape[1]
    per = map_ref.shape[1]
    total = slots * corners
    at = slots * rows
    moves = (
        (scale_hbm, scale_ref),
        (rhs_hbm, rhs_ref),
        (corner_hbm, corner_ref),
        (place_hbm, place_ref),
        (map_hbm, map_ref),
        (count_hbm, count_ref),
        (diag_hbm, diag_ref),
        (panel_hbm, panel_ref),
    )
    copies = [pltpu.make_async_copy(a, b, sems.at[i]) for i, (a, b) in enumerate(moves)]
    for copy in copies:
        copy.start()
    pack_ref[at:, :] = jnp.zeros((16, width), F32)
    rows_ref[...] = jnp.zeros_like(rows_ref)
    facts[...] = jnp.zeros_like(facts)
    for copy in copies:
        copy.wait()
    v_ref[...] = scale_ref[...] * rhs_ref[...]
    pack_ref[at + 8 : at + 8 + slots, :] = diag_ref[...]
    lane = iota((1, LANES), 1)
    for s in range(slots):
        pack_ref[s * rows : (s + 1) * rows, :] = panel_ref[s].astype(F32)
        rows_ref[s * corners : (s + 1) * corners, :] = corner_ref[s].astype(F32)
        facts[s : s + 1, :corners] = place_ref[s : s + 1, :].astype(F32)
        facts[slots + s : slots + s + 1, :per] = map_ref[s : s + 1, :].astype(F32)
    for i in range(total // 8):
        pack_ref[at : at + 8, i * LANES : (i + 1) * LANES] = rows_ref[8 * i : 8 * i + 8, :]
    narrow = rows_ref[...].astype(BF16)
    square = lax.dot_general(
        narrow, narrow, (((1,), (1,)), ((), ())), preferred_element_type=F32
    )
    part = jnp.zeros((corners, LANES), F32)
    count = count_ref[0, 0]
    fact = jnp.where(lane == total + slots * per, count.astype(F32), 0.0)
    for s in range(slots):
        live = jnp.where(s < count, 1.0, 0.0)
        first = s * corners
        mine = (lane >= first) & (lane < first + corners)
        part = jnp.where(mine, square[first : first + corners, :] * live, part)
        row = facts[s : s + 1, :]
        column = jnp.sum(
            jnp.where(iota((corners, 1), 0) == lane, row, 0.0), axis=1, keepdims=True
        )
        part = jnp.where(lane == total + s, column, part)
        fact = fact + (pltpu.roll(row, first, 1) if s else row)
        fact = fact + pltpu.roll(facts[slots + s : slots + s + 1, :], total + s * per, 1)
    report_ref[:corners, :] = part
    report_ref[corners:, :] = jnp.broadcast_to(fact, (8, LANES))
    facts_ref[...] = jnp.broadcast_to(fact.astype(jnp.int32), (8, LANES))


def flipped(a, b):
    return lax.dot_general(
        a, b, (((1,), (1,)), ((), ())), precision=lax.Precision.HIGHEST, preferred_element_type=F32
    )


def split_inverse(m, n):
    h = n // 2
    a, b, bt, c = m[:h, :h], m[:h, h:], m[h:, :h], m[h:, h:]
    ai = small_inverse(a, h)
    u = high(ai, b)
    si = small_inverse(c - high(bt, u), h)
    x, xt = high(u, si), flipped(si, u)
    top = jnp.concatenate([ai + flipped(x, u), -x], axis=1)
    return jnp.concatenate([top, jnp.concatenate([-xt, si], axis=1)], axis=0)


def coarse_kernel(
    slots, corners, start, y_ref, gathered_ref, diag_ref, out_ref, rows_ref, places_ref, facts_ref,
    hot_ref, spread_ref,
):
    count = gathered_ref.shape[0]
    total = slots * corners
    n = diag_ref.shape[1]
    lane = iota((1, n), 1).astype(F32)
    for y in range(count):
        part = gathered_ref[y, start : start + corners, :]
        rows_ref[y : y + 1, :] = gathered_ref[y, start + corners : start + corners + 1, :]
        for s in range(slots):
            block = part[:, s * corners : (s + 1) * corners]
            place = part[:, total + s : total + s + 1]
            hot = jnp.where(place == lane, 1.0, 0.0)
            at = (y * slots + s) * corners
            hot_ref[at : at + corners, :] = hot
            spread_ref[at : at + corners, :] = exact_times(block, hot.astype(BF16))
    facts_ref[...] = jnp.zeros_like(facts_ref)
    for g, by in enumerate((0, 1, -1)):
        there = y_ref[0] + by
        y = jnp.clip(there, 0, count - 1)
        fact = gathered_ref[y, start + corners : start + corners + 1, :].astype(jnp.int32)
        facts_ref[g : g + 1, :] = jnp.where((there >= 0) & (there < count), fact, 0)
        part = gathered_ref[y, start : start + corners, :]
        for s in range(slots):
            at = g * total + s * corners
            places_ref[at : at + corners, :] = jnp.broadcast_to(
                part[:, total + s : total + s + 1], (corners, LANES)
            )
    hots = hot_ref[...].astype(BF16)
    system = jnp.where(iota((n, 1), 0) == iota((1, n), 1), diag_ref[...], 0.0)
    for piece in thirds(spread_ref[...]):
        system = system + lax.dot_general(
            hots, piece.astype(BF16), (((0,), (0,)), ((), ())), preferred_element_type=F32
        )
    out_ref[...] = system
    b = LANES

    def eliminate(k, carry):
        ro = pl.multiple_of(k * b, b)
        pivots = split_inverse(out_ref[pl.ds(ro, b), pl.ds(ro, b)], b)
        col = out_ref[:, pl.ds(ro, b)]
        out_ref[:, pl.ds(ro, b)] = jnp.zeros((n, b), F32)
        out_ref[pl.ds(ro, b), pl.ds(ro, b)] = jnp.where(iota((b, b), 0) == iota((b, b), 1), 1.0, 0.0)
        fresh = high(pivots, out_ref[pl.ds(ro, b), :])
        out_ref[pl.ds(ro, b), :] = jnp.zeros((b, n), F32)
        at = iota((n, 1), 0)
        others = jnp.where((at >= ro) & (at < ro + b), 0.0, col)
        out_ref[...] = out_ref[...] - high(others, fresh)
        out_ref[pl.ds(ro, b), :] = fresh
        return carry

    lax.fori_loop(0, n // b, eliminate, 0)


def fact_of(facts, slots, corners, per, g, s, b, owned):
    k = facts[g, slots * corners + s * per + b]
    live = jnp.where(s < facts[g, slots * corners + slots * per], 1.0, 0.0)
    return k, jnp.where(k < owned, live, -live)


def gathered_rows(slots, corners, per, owned, g, facts, cand, u_ref):
    for s in range(slots):
        for b in range(per):
            k, sign = fact_of(facts, slots, corners, per, g, s, b, owned)
            row = cand[pl.ds(g * 5 * owned + k, 1), :] * sign
            u_ref[g * slots + s : g * slots + s + 1, b * LANES : (b + 1) * LANES] = row


def before_kernel(slots, corners, per, sweep, groups, parts, v_ref, last_ref, corner_ref, facts_ref, *rest):
    rest, (pay_ref, cand, u_ref, facts, sem) = rest[:-5], rest[-5:]
    packs, halo, extra = rest[:groups], rest[groups : groups + parts], rest[groups + parts :]
    copy = pltpu.make_async_copy(facts_ref, facts, sem)
    copy.start()
    owned = v_ref.shape[0]
    total = slots * corners
    v = v_ref[...]
    if groups > 1:
        cand[...] = jnp.zeros_like(cand)
        cand[9 * owned : 10 * owned, :] = v
        cand[13 * owned : 14 * owned, :] = v
    for i, ref in enumerate((v_ref, *halo)):
        cand[i * owned : (i + 1) * owned, :] = ref[...]
        if i < 3:
            pay_ref[i * owned : (i + 1) * owned, :] = ref[...]
    at = iota((owned, 1), 0)
    lane = iota((1, LANES), 1)
    energy = jnp.sum(v * v, keepdims=True)
    pays = []
    copy.wait()
    for g in range(groups):
        pack = packs[g]
        rows = (pack.shape[0] - 16) // slots
        pay = jnp.zeros((1, LANES), F32)
        gathered_rows(slots, corners, per, owned, g, facts, cand, u_ref)
        for s in range(slots):
            live = jnp.where(s < facts[g, total + slots * per], 1.0, 0.0)
            u = u_ref[g * slots + s : g * slots + s + 1, :]
            t = row_times(u, pack[s * rows : (s + 1) * rows, :].astype(BF16), 1)
            energy = energy + jnp.sum(t * t, keepdims=True)
            weights = pack[slots * rows + 8 + s : slots * rows + 9 + s, :]
            energy = energy + jnp.sum(weights * u * u, keepdims=True)
            first = s * corners
            if g:
                j = slots * rows
                narrow = [
                    pack[j : j + 8, i * LANES : (i + 1) * LANES] for i in range(total // 8)
                ]
                narrow = jnp.concatenate(narrow + [jnp.zeros((LANES - total, LANES), F32)], axis=0)
            else:
                narrow = corner_ref[...]
            c = row_times(t, narrow.astype(BF16), 1) * live
            pay = jnp.where((lane >= first) & (lane < first + corners), c, pay)
        pays.append(pay)
    cross = jnp.sum(v * last_ref[...], keepdims=True)
    pay = pays[0]
    if groups == 1:
        pay = jnp.where(lane == total + 2 * sweep, energy, pay)
    pay = jnp.where(lane == total + 2 * sweep + 1, cross, pay)
    for ref in extra:
        if ref.shape[0] == 1:
            pay = pay + ref[...]
        else:
            pay_ref[4 * owned :, :] = ref[...]
    block = jnp.where(at == 0, pay, 0.0)
    for g in range(1, groups):
        block = jnp.where(at == g, pays[g], block)
    pay_ref[3 * owned : 4 * owned, :] = block


def after_kernel(
    slots, corners, per, sweep, partial, y_ref, gathered_ref, rows_ref, places_ref, facts_ref, inverse_ref,
    *rest,
):
    packs, rest = rest[:3], rest[3:]
    before, rest = rest[: 1 if sweep else 0], rest[1 if sweep else 0 :]
    late, (cand, u_ref, acc, facts, sem) = rest[4:-5], rest[-5:]
    mine, east, west, sums_ref = rest[:4]
    copy = pltpu.make_async_copy(facts_ref, facts, sem)
    copy.start()
    owned = mine.shape[0]
    total = slots * corners
    n = inverse_ref.shape[0]
    count = gathered_ref.shape[0]
    middle = y_ref[0]
    field = {}
    for by in (0, 1, -1, 2, -2):
        y = middle + by
        inside = jnp.where((y >= 0) & (y < count), 1.0, 0.0)
        p = jnp.clip(y, 0, count - 1)
        for i in range(3 if abs(by) < 2 else 1):
            field[by, i] = gathered_ref[p, i * owned : (i + 1) * owned, :] * inside
    for g, by in enumerate((0, 1, -1)):
        parts = (field[by, 0], field[by, 1], field[by, 2])
        parts += (field[by + 1, 0] if by < 2 else None, field[by - 1, 0])
        for i, part in enumerate(parts):
            at = (5 * g + i) * owned
            cand[at : at + owned, :] = part
    lane = iota((1, LANES), 1)
    at = iota((n, 1), 0)
    spread = jnp.zeros((n, LANES), F32)
    totals = jnp.zeros((1, LANES), F32)
    places = rows_ref[...].astype(jnp.int32)
    for p in range(count):
        row = gathered_ref[p, 3 * owned : 3 * owned + 1, :]
        if partial and p > 0:
            row = row + gathered_ref[p - 1, 3 * owned + 1 : 3 * owned + 2, :]
        if partial and p < count - 1:
            row = row + gathered_ref[p + 1, 3 * owned + 2 : 3 * owned + 3, :]
        totals = totals + row
        spread = spread + jnp.where(places[p : p + 1, :] == at, row, 0.0)
    right = jnp.sum(jnp.where(lane < total, spread, 0.0), axis=1, keepdims=True)
    coarse = jnp.sum(inverse_ref[...] * right, axis=0, keepdims=True)
    wide = iota((1, n), 1)
    right_row = jnp.sum(jnp.where(at == wide, right, 0.0), axis=0, keepdims=True)
    energy = jnp.sum(coarse * right_row, keepdims=True)
    totals = totals + jnp.where(lane == total + 2 * sweep, energy, 0.0)
    for ref in before:
        totals = totals + ref[...]
    sums_ref[...] = totals
    acc[...] = jnp.zeros_like(acc)
    acc[:owned, :] = field[0, 0]
    copy.wait()
    for g in range(3):
        gathered_rows(slots, corners, per, owned, g, facts, cand, u_ref)
    wide = wide.astype(F32)
    local = jnp.sum(field[0, 0] * field[0, 0], keepdims=True)
    for g in range(3):
        pack = packs[g]
        rows = (pack.shape[0] - 16) // slots
        tail = slots * rows
        for s in range(slots):
            panel = pack[s * rows : (s + 1) * rows, :].astype(BF16)
            u = u_ref[g * slots + s : g * slots + s + 1, :]
            t = row_times(u, panel, 1)
            weights = pack[tail + 8 + s : tail + 9 + s, :]
            if g == 0:
                local = local + jnp.sum(t * t, keepdims=True)
                local = local + jnp.sum(weights * u * u, keepdims=True)
            for i in range(corners // 8):
                first = s * corners + 8 * i
                place = places_ref[g * total + first : g * total + first + 8, :1]
                back = jnp.sum(jnp.where(place == wide, coarse, 0.0), axis=1, keepdims=True)
                j = first // 8
                part = pack[tail : tail + 8, j * LANES : (j + 1) * LANES]
                t = t + jnp.sum(back * part, axis=0, keepdims=True)
            w = row_times(t, panel, 0) + weights * u
            for b in range(per):
                k, sign = fact_of(facts, slots, corners, per, g, s, b, owned)
                acc[pl.ds(g * 5 * owned + k, 1), :] += w[:, b * LANES : (b + 1) * LANES] * sign
    mine[...] = acc[:owned, :] + acc[9 * owned : 10 * owned, :] + acc[13 * owned : 14 * owned, :]
    for ref in late:
        ref[...] = jnp.where(lane == total + 2 * sweep, local, 0.0)
    east[...] = acc[owned : 2 * owned, :]
    west[...] = acc[2 * owned : 3 * owned, :]


def final_kernel(first, gathered_ref, rhs_ref, v0, v1, v2, w0, w1, mine, east, west, x_ref, r_ref):
    sums = gathered_ref[...]
    lane = iota((1, LANES), 1)

    def moment(i):
        return jnp.sum(jnp.where(lane == first + i, sums, 0.0), axis=1, keepdims=True)

    h00, r0, h11, h01, h22, h12 = (moment(i) for i in range(6))
    h02, r1, r2 = h11, STEP * h00, STEP * h01
    l10, l20 = h01 / h00, h02 / h00
    d1 = h11 - l10 * h01
    e12 = h12 - l10 * h02
    l21 = e12 / d1
    d2 = h22 - l20 * h02 - l21 * e12
    y1 = r1 - l10 * r0
    y2 = r2 - l20 * r0 - l21 * y1
    c2 = y2 / d2
    c1 = y1 / d1 - l21 * c2
    c0 = r0 / h00 - l10 * c1 - l20 * c2
    w2 = mine[...] + east[...] + west[...]
    x_ref[...] = c0 * v0[...] + c1 * v1[...] + c2 * v2[...]
    r_ref[...] = rhs_ref[...] - (c0 * w0[...] + c1 * w1[...] + c2 * w2)


def call(kernel, name, outs, scratch, scalars, arrays, space=pltpu.VMEM):
    vmem = pl.BlockSpec(memory_space=pltpu.VMEM)
    smem = pl.BlockSpec(memory_space=pltpu.SMEM)
    outs = [x if isinstance(x, jax.ShapeDtypeStruct) else jax.ShapeDtypeStruct(x, F32) for x in outs]
    return pl.pallas_call(
        kernel,
        out_shape=outs,
        in_specs=[smem] * len(scalars) + [pl.BlockSpec(memory_space=space)] * len(arrays),
        out_specs=[vmem] * len(outs),
        scratch_shapes=[pltpu.VMEM(x, F32) if isinstance(x, tuple) else x for x in scratch],
        compiler_params=pltpu.CompilerParams(vmem_limit_bytes=40 << 20),
        name=name,
    )(*scalars, *arrays)


def moved(x, axis, by):
    count = lax.axis_size(axis)
    return lax.ppermute(x, axis, [(i, i + by) for i in range(count) if 0 <= i + by < count])


def strided(count, by):
    return [list(range(i, count, by)) for i in range(by)]


def runs(count, size):
    return [list(range(i, i + size)) for i in range(0, count, size)]


def shards(
    panel, corner_panel, interface_diag, coarse_diag, scaling, dual_rhs, block_map, corner_map, counts
):
    slots, rows, width = panel.shape[2:]
    corners = corner_panel.shape[3]
    owned, block_size = scaling.shape[2:]
    n = coarse_diag.shape[1]
    total = slots * corners
    peers = lax.axis_size("gy")
    y = lax.axis_index("gy")
    per = block_map.shape[3]
    tile = (owned, block_size)
    facts_shape = jax.ShapeDtypeStruct((8, LANES), jnp.int32)
    facts_scratch = [pltpu.SMEM((8, LANES), jnp.int32), pltpu.SemaphoreType.DMA]
    direction, scale, rhs, pack, report, corner_rows, facts = call(
        setup_kernel,
        "setup",
        [
            tile,
            tile,
            tile,
            (slots * rows + 16, width),
            (corners + 8, LANES),
            (LANES, LANES),
            facts_shape,
        ],
        [
            pltpu.VMEM((slots, rows, width), BF16),
            pltpu.VMEM((slots, corners, rows), BF16),
            (slots, width),
            pltpu.VMEM((slots, corners), jnp.int32),
            pltpu.VMEM((slots, per), jnp.int32),
            pltpu.SMEM((1, 1), jnp.int32),
            (8, LANES),
            pltpu.SemaphoreType.DMA((8,)),
        ],
        [],
        [
            panel[0, 0],
            corner_panel[0, 0],
            interface_diag[0, 0],
            corner_map[0, 0],
            block_map[0, 0],
            counts,
            scaling[0, 0],
            dual_rhs[0, 0],
        ],
        space=pltpu.HBM,
    )
    last = rhs
    directions, images, sums = [], [], []
    packs, late = [pack], []
    for sweep in range(3):
        partial = sweep == 1
        halo = [moved(direction, "gx", -1), moved(direction, "gx", 1)]
        if not partial:
            halo += [moved(direction, "gy", -1), moved(direction, "gy", 1)]
        extra = late if sweep else [report]
        size = 4 * owned + (0 if sweep else report.shape[0])
        groups = 3 if partial else 1
        (pay,) = call(
            functools.partial(before_kernel, slots, corners, per, sweep, groups, len(halo)),
            "before",
            [(size, LANES)],
            [(5 * groups * owned, block_size), (8, width), *facts_scratch],
            [],
            [
                direction,
                last,
                corner_rows,
                facts3 if partial else facts,
                *packs[:groups],
                *halo,
                *extra,
            ],
        )
        gathered = lax.all_gather(pay, "gy")
        if not sweep:
            gathered, leaving = lax.optimization_barrier((gathered, pack))
            packs = [pack, moved(leaving, "gy", -1), moved(leaving, "gy", 1)]
            here = y.reshape(1).astype(jnp.int32)
            inverse, place_rows, places3, facts3 = call(
                functools.partial(coarse_kernel, slots, corners, 4 * owned),
                "coarse",
                [(n, n), (peers, LANES), (3 * total, LANES), facts_shape],
                [(peers * total, n), (peers * total, n)],
                [here],
                [gathered, coarse_diag],
            )
        mine, east, west, sums, *late = call(
            functools.partial(after_kernel, slots, corners, per, sweep, partial),
            "after",
            [tile] * 3 + [(1, LANES)] * (2 if partial else 1),
            [(15 * owned, block_size), (8, width), (15 * owned, block_size), *facts_scratch],
            [here],
            [gathered, place_rows, places3, facts3, inverse, *packs, *([sums] if sweep else [])],
        )
        arrived = [moved(east, "gx", 1), moved(west, "gx", -1)]
        directions.append(direction)
        if sweep < 2:
            image = mine + arrived[0] + arrived[1]
            images.append(image)
            last, direction = image, STEP * scale * image
    sums, *arrived = lax.optimization_barrier((sums, *arrived))
    across = lax.axis_size("gx")
    for group in (runs(across, 4), strided(across, 4)):
        sums = lax.all_gather(sums, "gx", axis=0, tiled=True, axis_index_groups=group)
        sums = jnp.sum(sums, axis=0, keepdims=True)
    multipliers, residual = call(
        functools.partial(final_kernel, total),
        "final",
        [tile] * 2,
        [],
        [],
        [sums, rhs, *directions, *images, mine, *arrived],
    )
    return multipliers[None, None], residual[None, None]


def solution(mesh):
    return jax.shard_map(
        shards,
        mesh=mesh,
        in_specs=(
            P("gx", "gy", None, None, None),
            P("gx", "gy", None, None, None),
            P("gx", "gy", None, None),
            P("gx", None),
            P("gx", "gy", None, None),
            P("gx", "gy", None, None),
            P("gx", "gy", None, None),
            P("gx", "gy", None, None),
            P("gx", "gy"),
        ),
        out_specs=(P("gx", "gy", None, None), P("gx", "gy", None, None)),
        check_vma=False,
    )
```

```python
import functools

import jax
import jax.numpy as jnp
from jax import lax
from jax.experimental import pallas as pl
from jax.experimental.pallas import tpu as pltpu
from jax.sharding import PartitionSpec as P

F32 = jnp.float32
BF16 = jnp.bfloat16
STEP = 0.00390625
LANES = 128
PIVOTS = 4


def iota(shape, dim):
    return lax.broadcasted_iota(jnp.int32, shape, dim)


def high(a, b):
    return jnp.dot(a, b, precision=lax.Precision.HIGHEST, preferred_element_type=F32)


def thirds(x):
    first = x.astype(BF16).astype(F32)
    rest = x - first
    second = rest.astype(BF16).astype(F32)
    return first, second, rest - second


def stacked(row):
    first, second, third = thirds(row)
    at = iota((16, 1), 0)
    rows = jnp.where(at == 0, first, jnp.where(at == 1, second, jnp.where(at == 2, third, 0.0)))
    return rows.astype(BF16)


def row_times(row, matrix, dim):
    out = lax.dot_general(
        stacked(row), matrix, (((1,), (dim,)), ((), ())), preferred_element_type=F32
    )
    return jnp.sum(out[:8], axis=0, keepdims=True)


def exact_times(x, hot):
    return sum(jnp.dot(piece.astype(BF16), hot, preferred_element_type=F32) for piece in thirds(x))


def inverse2(a, b, c):
    r = 1.0 / (a * c - b * b)
    return c * r, -b * r, a * r


def pivot_inverse(e):
    p = inverse2(e(0, 0), e(0, 1), e(1, 1))
    b = [[e(0, 2), e(0, 3)], [e(1, 2), e(1, 3)]]
    u = [
        [p[0] * b[0][j] + p[1] * b[1][j] for j in (0, 1)],
        [p[1] * b[0][j] + p[2] * b[1][j] for j in (0, 1)],
    ]
    s = inverse2(
        e(2, 2) - (b[0][0] * u[0][0] + b[1][0] * u[1][0]),
        e(2, 3) - (b[0][0] * u[0][1] + b[1][0] * u[1][1]),
        e(3, 3) - (b[0][1] * u[0][1] + b[1][1] * u[1][1]),
    )
    x = [[u[i][0] * s[0] + u[i][1] * s[1], u[i][0] * s[1] + u[i][1] * s[2]] for i in (0, 1)]
    p00 = p[0] + x[0][0] * u[0][0] + x[0][1] * u[0][1]
    p01 = p[1] + x[0][0] * u[1][0] + x[0][1] * u[1][1]
    p11 = p[2] + x[1][0] * u[1][0] + x[1][1] * u[1][1]
    return [
        [p00, p01, -x[0][0], -x[0][1]],
        [p01, p11, -x[1][0], -x[1][1]],
        [-x[0][0], -x[1][0], s[0], s[1]],
        [-x[0][1], -x[1][1], s[1], s[2]],
    ]


def small_inverse(a, n):
    lane = iota((1, n), 1)
    at8 = iota((8, 1), 0)
    for k in range(0, n, PIVOTS):
        rows = [a[k + i : k + i + 1, :] for i in range(PIVOTS)]
        cols = [jnp.broadcast_to(a[:, k + i : k + i + 1], (n, n)) for i in range(PIVOTS)]
        w = pivot_inverse(lambda i, j: cols[j][k + i : k + i + 1, :])
        inside = (lane >= k) & (lane < k + PIVOTS)
        units = [
            jnp.where(inside, jnp.where(lane == k + i, 1.0, 0.0), rows[i]) for i in range(PIVOTS)
        ]
        fresh = [sum(w[i][j] * units[j] for j in range(PIVOTS)) for i in range(PIVOTS)]
        base = jnp.where(inside, 0.0, a)
        for i in range(PIVOTS):
            base = base - cols[i] * fresh[i]
        v = k // 8 * 8
        block = base[v : v + 8]
        for i in range(PIVOTS):
            block = jnp.where(at8 == k + i - v, fresh[i], block)
        a = jnp.concatenate([x for x in (base[:v], block, base[v + 8 :]) if x.shape[0]], axis=0)
    return a


def setup_kernel(
    panel_hbm, corner_hbm, diag_hbm, place_hbm, map_hbm, count_hbm, pack_ref, report_ref, rows_ref, facts_ref, panel_ref, corner_ref, diag_ref,
    place_ref, map_ref, count_ref, facts, sems,
):
    slots, rows, width = panel_ref.shape
    corners = corner_ref.shape[1]
    per = map_ref.shape[1]
    total = slots * corners
    at = slots * rows
    moves = (
        (corner_hbm, corner_ref),
        (place_hbm, place_ref),
        (map_hbm, map_ref),
        (count_hbm, count_ref),
        (diag_hbm, diag_ref),
        (panel_hbm, panel_ref),
    )
    copies = [pltpu.make_async_copy(a, b, sems.at[i]) for i, (a, b) in enumerate(moves)]
    for copy in copies:
        copy.start()
    pack_ref[at:, :] = jnp.zeros((16, width), F32)
    rows_ref[...] = jnp.zeros_like(rows_ref)
    facts[...] = jnp.zeros_like(facts)
    for copy in copies:
        copy.wait()
    pack_ref[at + 8 : at + 8 + slots, :] = diag_ref[...]
    lane = iota((1, LANES), 1)
    for s in range(slots):
        pack_ref[s * rows : (s + 1) * rows, :] = panel_ref[s].astype(F32)
        rows_ref[s * corners : (s + 1) * corners, :] = corner_ref[s].astype(F32)
        facts[s : s + 1, :corners] = place_ref[s : s + 1, :].astype(F32)
        facts[slots + s : slots + s + 1, :per] = map_ref[s : s + 1, :].astype(F32)
    for i in range(total // 8):
        pack_ref[at : at + 8, i * LANES : (i + 1) * LANES] = rows_ref[8 * i : 8 * i + 8, :]
    narrow = rows_ref[...].astype(BF16)
    square = lax.dot_general(
        narrow, narrow, (((1,), (1,)), ((), ())), preferred_element_type=F32
    )
    part = jnp.zeros((corners, LANES), F32)
    count = count_ref[0, 0]
    fact = jnp.where(lane == total + slots * per, count.astype(F32), 0.0)
    for s in range(slots):
        live = jnp.where(s < count, 1.0, 0.0)
        first = s * corners
        mine = (lane >= first) & (lane < first + corners)
        part = jnp.where(mine, square[first : first + corners, :] * live, part)
        row = facts[s : s + 1, :]
        column = jnp.sum(
            jnp.where(iota((corners, 1), 0) == lane, row, 0.0), axis=1, keepdims=True
        )
        part = jnp.where(lane == total + s, column, part)
        fact = fact + (pltpu.roll(row, first, 1) if s else row)
        fact = fact + pltpu.roll(facts[slots + s : slots + s + 1, :], total + s * per, 1)
    report_ref[:corners, :] = part
    report_ref[corners:, :] = jnp.broadcast_to(fact, (8, LANES))
    facts_ref[...] = jnp.broadcast_to(fact.astype(jnp.int32), (8, LANES))


def flipped(a, b):
    return lax.dot_general(
        a, b, (((1,), (1,)), ((), ())), precision=lax.Precision.HIGHEST, preferred_element_type=F32
    )


def split_inverse(m, n):
    h = n // 2
    a, b, bt, c = m[:h, :h], m[:h, h:], m[h:, :h], m[h:, h:]
    ai = small_inverse(a, h)
    u = high(ai, b)
    si = small_inverse(c - high(bt, u), h)
    x, xt = high(u, si), flipped(si, u)
    top = jnp.concatenate([ai + flipped(x, u), -x], axis=1)
    return jnp.concatenate([top, jnp.concatenate([-xt, si], axis=1)], axis=0)


def coarse_kernel(
    slots, corners, start, y_ref, gathered_ref, diag_ref, out_ref, rows_ref, places_ref, facts_ref,
    hot_ref, spread_ref,
):
    count = gathered_ref.shape[0]
    total = slots * corners
    n = diag_ref.shape[1]
    lane = iota((1, n), 1).astype(F32)
    for y in range(count):
        part = gathered_ref[y, start : start + corners, :]
        rows_ref[y : y + 1, :] = gathered_ref[y, start + corners : start + corners + 1, :]
        for s in range(slots):
            block = part[:, s * corners : (s + 1) * corners]
            place = part[:, total + s : total + s + 1]
            hot = jnp.where(place == lane, 1.0, 0.0)
            at = (y * slots + s) * corners
            hot_ref[at : at + corners, :] = hot
            spread_ref[at : at + corners, :] = exact_times(block, hot.astype(BF16))
    facts_ref[...] = jnp.zeros_like(facts_ref)
    for g, by in enumerate((0, 1, -1)):
        there = y_ref[0] + by
        y = jnp.clip(there, 0, count - 1)
        fact = gathered_ref[y, start + corners : start + corners + 1, :].astype(jnp.int32)
        facts_ref[g : g + 1, :] = jnp.where((there >= 0) & (there < count), fact, 0)
        part = gathered_ref[y, start : start + corners, :]
        for s in range(slots):
            at = g * total + s * corners
            places_ref[at : at + corners, :] = jnp.broadcast_to(
                part[:, total + s : total + s + 1], (corners, LANES)
            )
    hots = hot_ref[...].astype(BF16)
    system = jnp.where(iota((n, 1), 0) == iota((1, n), 1), diag_ref[...], 0.0)
    for piece in thirds(spread_ref[...]):
        system = system + lax.dot_general(
            hots, piece.astype(BF16), (((0,), (0,)), ((), ())), preferred_element_type=F32
        )
    out_ref[...] = system
    b = LANES

    def eliminate(k, carry):
        ro = pl.multiple_of(k * b, b)
        pivots = split_inverse(out_ref[pl.ds(ro, b), pl.ds(ro, b)], b)
        col = out_ref[:, pl.ds(ro, b)]
        out_ref[:, pl.ds(ro, b)] = jnp.zeros((n, b), F32)
        out_ref[pl.ds(ro, b), pl.ds(ro, b)] = jnp.where(iota((b, b), 0) == iota((b, b), 1), 1.0, 0.0)
        fresh = high(pivots, out_ref[pl.ds(ro, b), :])
        out_ref[pl.ds(ro, b), :] = jnp.zeros((b, n), F32)
        at = iota((n, 1), 0)
        others = jnp.where((at >= ro) & (at < ro + b), 0.0, col)
        out_ref[...] = out_ref[...] - high(others, fresh)
        out_ref[pl.ds(ro, b), :] = fresh
        return carry

    lax.fori_loop(0, n // b, eliminate, 0)


def fact_of(facts, slots, corners, per, g, s, b, owned):
    k = facts[g, slots * corners + s * per + b]
    live = jnp.where(s < facts[g, slots * corners + slots * per], 1.0, 0.0)
    return k, jnp.where(k < owned, live, -live)


def gathered_rows(slots, corners, per, owned, g, facts, cand, u_ref):
    for s in range(slots):
        for b in range(per):
            k, sign = fact_of(facts, slots, corners, per, g, s, b, owned)
            row = cand[pl.ds(g * 5 * owned + k, 1), :] * sign
            u_ref[g * slots + s : g * slots + s + 1, b * LANES : (b + 1) * LANES] = row


def before_kernel(slots, corners, per, sweep, groups, parts, v_ref, last_ref, corner_ref, facts_ref, *rest):
    rest, (pay_ref, cand, u_ref, facts, sem) = rest[:-5], rest[-5:]
    packs, halo, extra = rest[:groups], rest[groups : groups + parts], rest[groups + parts :]
    copy = pltpu.make_async_copy(facts_ref, facts, sem)
    copy.start()
    owned = v_ref.shape[0]
    total = slots * corners
    v = v_ref[...]
    if groups > 1:
        cand[...] = jnp.zeros_like(cand)
        cand[9 * owned : 10 * owned, :] = v
        cand[13 * owned : 14 * owned, :] = v
    for i, ref in enumerate((v_ref, *halo)):
        cand[i * owned : (i + 1) * owned, :] = ref[...]
        if i < 3:
            pay_ref[i * owned : (i + 1) * owned, :] = ref[...]
    at = iota((owned, 1), 0)
    lane = iota((1, LANES), 1)
    energy = jnp.sum(v * v, keepdims=True)
    pays = []
    copy.wait()
    for g in range(groups):
        pack = packs[g]
        rows = (pack.shape[0] - 16) // slots
        pay = jnp.zeros((1, LANES), F32)
        gathered_rows(slots, corners, per, owned, g, facts, cand, u_ref)
        for s in range(slots):
            live = jnp.where(s < facts[g, total + slots * per], 1.0, 0.0)
            u = u_ref[g * slots + s : g * slots + s + 1, :]
            t = row_times(u, pack[s * rows : (s + 1) * rows, :].astype(BF16), 1)
            energy = energy + jnp.sum(t * t, keepdims=True)
            weights = pack[slots * rows + 8 + s : slots * rows + 9 + s, :]
            energy = energy + jnp.sum(weights * u * u, keepdims=True)
            first = s * corners
            if g:
                j = slots * rows
                narrow = [
                    pack[j : j + 8, i * LANES : (i + 1) * LANES] for i in range(total // 8)
                ]
                narrow = jnp.concatenate(narrow + [jnp.zeros((LANES - total, LANES), F32)], axis=0)
            else:
                narrow = corner_ref[...]
            c = row_times(t, narrow.astype(BF16), 1) * live
            pay = jnp.where((lane >= first) & (lane < first + corners), c, pay)
        pays.append(pay)
    cross = jnp.sum(v * last_ref[...], keepdims=True)
    pay = pays[0]
    if groups == 1:
        pay = jnp.where(lane == total + 2 * sweep, energy, pay)
    pay = jnp.where(lane == total + 2 * sweep + 1, cross, pay)
    for ref in extra:
        if ref.shape[0] == 1:
            pay = pay + ref[...]
        else:
            pay_ref[4 * owned :, :] = ref[...]
    block = jnp.where(at == 0, pay, 0.0)
    for g in range(1, groups):
        block = jnp.where(at == g, pays[g], block)
    pay_ref[3 * owned : 4 * owned, :] = block


def after_kernel(
    slots, corners, per, sweep, partial, y_ref, gathered_ref, rows_ref, places_ref, facts_ref, inverse_ref,
    *rest,
):
    packs, rest = rest[:3], rest[3:]
    before, rest = rest[: 1 if sweep else 0], rest[1 if sweep else 0 :]
    late, (cand, u_ref, acc, facts, sem) = rest[4:-5], rest[-5:]
    mine, east, west, sums_ref = rest[:4]
    copy = pltpu.make_async_copy(facts_ref, facts, sem)
    copy.start()
    owned = mine.shape[0]
    total = slots * corners
    n = inverse_ref.shape[0]
    count = gathered_ref.shape[0]
    middle = y_ref[0]
    field = {}
    for by in (0, 1, -1, 2, -2):
        y = middle + by
        inside = jnp.where((y >= 0) & (y < count), 1.0, 0.0)
        p = jnp.clip(y, 0, count - 1)
        for i in range(3 if abs(by) < 2 else 1):
            field[by, i] = gathered_ref[p, i * owned : (i + 1) * owned, :] * inside
    for g, by in enumerate((0, 1, -1)):
        parts = (field[by, 0], field[by, 1], field[by, 2])
        parts += (field[by + 1, 0] if by < 2 else None, field[by - 1, 0])
        for i, part in enumerate(parts):
            at = (5 * g + i) * owned
            cand[at : at + owned, :] = part
    lane = iota((1, LANES), 1)
    at = iota((n, 1), 0)
    spread = jnp.zeros((n, LANES), F32)
    totals = jnp.zeros((1, LANES), F32)
    places = rows_ref[...].astype(jnp.int32)
    for p in range(count):
        row = gathered_ref[p, 3 * owned : 3 * owned + 1, :]
        if partial and p > 0:
            row = row + gathered_ref[p - 1, 3 * owned + 1 : 3 * owned + 2, :]
        if partial and p < count - 1:
            row = row + gathered_ref[p + 1, 3 * owned + 2 : 3 * owned + 3, :]
        totals = totals + row
        spread = spread + jnp.where(places[p : p + 1, :] == at, row, 0.0)
    right = jnp.sum(jnp.where(lane < total, spread, 0.0), axis=1, keepdims=True)
    coarse = jnp.sum(inverse_ref[...] * right, axis=0, keepdims=True)
    wide = iota((1, n), 1)
    right_row = jnp.sum(jnp.where(at == wide, right, 0.0), axis=0, keepdims=True)
    energy = jnp.sum(coarse * right_row, keepdims=True)
    totals = totals + jnp.where(lane == total + 2 * sweep, energy, 0.0)
    for ref in before:
        totals = totals + ref[...]
    sums_ref[...] = totals
    acc[...] = jnp.zeros_like(acc)
    acc[:owned, :] = field[0, 0]
    copy.wait()
    for g in range(3):
        gathered_rows(slots, corners, per, owned, g, facts, cand, u_ref)
    wide = wide.astype(F32)
    local = jnp.sum(field[0, 0] * field[0, 0], keepdims=True)
    for g in range(3):
        pack = packs[g]
        rows = (pack.shape[0] - 16) // slots
        tail = slots * rows
        for s in range(slots):
            panel = pack[s * rows : (s + 1) * rows, :].astype(BF16)
            u = u_ref[g * slots + s : g * slots + s + 1, :]
            t = row_times(u, panel, 1)
            weights = pack[tail + 8 + s : tail + 9 + s, :]
            if g == 0:
                local = local + jnp.sum(t * t, keepdims=True)
                local = local + jnp.sum(weights * u * u, keepdims=True)
            for i in range(corners // 8):
                first = s * corners + 8 * i
                place = places_ref[g * total + first : g * total + first + 8, :1]
                back = jnp.sum(jnp.where(place == wide, coarse, 0.0), axis=1, keepdims=True)
                j = first // 8
                part = pack[tail : tail + 8, j * LANES : (j + 1) * LANES]
                t = t + jnp.sum(back * part, axis=0, keepdims=True)
            w = row_times(t, panel, 0) + weights * u
            for b in range(per):
                k, sign = fact_of(facts, slots, corners, per, g, s, b, owned)
                acc[pl.ds(g * 5 * owned + k, 1), :] += w[:, b * LANES : (b + 1) * LANES] * sign
    mine[...] = acc[:owned, :] + acc[9 * owned : 10 * owned, :] + acc[13 * owned : 14 * owned, :]
    for ref in late:
        ref[...] = jnp.where(lane == total + 2 * sweep, local, 0.0)
    east[...] = acc[owned : 2 * owned, :]
    west[...] = acc[2 * owned : 3 * owned, :]


def final_kernel(first, gathered_ref, rhs_ref, v0, v1, v2, w0, w1, mine, east, west, x_ref, r_ref):
    sums = gathered_ref[...]
    lane = iota((1, LANES), 1)

    def moment(i):
        return jnp.sum(jnp.where(lane == first + i, sums, 0.0), axis=1, keepdims=True)

    h00, r0, h11, h01, h22, h12 = (moment(i) for i in range(6))
    h02, r1, r2 = h11, STEP * h00, STEP * h01
    l10, l20 = h01 / h00, h02 / h00
    d1 = h11 - l10 * h01
    e12 = h12 - l10 * h02
    l21 = e12 / d1
    d2 = h22 - l20 * h02 - l21 * e12
    y1 = r1 - l10 * r0
    y2 = r2 - l20 * r0 - l21 * y1
    c2 = y2 / d2
    c1 = y1 / d1 - l21 * c2
    c0 = r0 / h00 - l10 * c1 - l20 * c2
    w2 = mine[...] + east[...] + west[...]
    x_ref[...] = c0 * v0[...] + c1 * v1[...] + c2 * v2[...]
    r_ref[...] = rhs_ref[...] - (c0 * w0[...] + c1 * w1[...] + c2 * w2)


def call(kernel, name, outs, scratch, scalars, arrays, space=pltpu.VMEM):
    vmem = pl.BlockSpec(memory_space=pltpu.VMEM)
    smem = pl.BlockSpec(memory_space=pltpu.SMEM)
    outs = [x if isinstance(x, jax.ShapeDtypeStruct) else jax.ShapeDtypeStruct(x, F32) for x in outs]
    return pl.pallas_call(
        kernel,
        out_shape=outs,
        in_specs=[smem] * len(scalars) + [pl.BlockSpec(memory_space=space)] * len(arrays),
        out_specs=[vmem] * len(outs),
        scratch_shapes=[pltpu.VMEM(x, F32) if isinstance(x, tuple) else x for x in scratch],
        compiler_params=pltpu.CompilerParams(vmem_limit_bytes=40 << 20),
        name=name,
    )(*scalars, *arrays)


def moved(x, axis, by):
    count = lax.axis_size(axis)
    return lax.ppermute(x, axis, [(i, i + by) for i in range(count) if 0 <= i + by < count])


def strided(count, by):
    return [list(range(i, count, by)) for i in range(by)]


def runs(count, size):
    return [list(range(i, i + size)) for i in range(0, count, size)]


def shards(
    panel, corner_panel, interface_diag, coarse_diag, scaling, dual_rhs, block_map, corner_map, counts
):
    slots, rows, width = panel.shape[2:]
    corners = corner_panel.shape[3]
    owned, block_size = scaling.shape[2:]
    n = coarse_diag.shape[1]
    total = slots * corners
    peers = lax.axis_size("gy")
    y = lax.axis_index("gy")
    per = block_map.shape[3]
    tile = (owned, block_size)
    facts_shape = jax.ShapeDtypeStruct((8, LANES), jnp.int32)
    facts_scratch = [pltpu.SMEM((8, LANES), jnp.int32), pltpu.SemaphoreType.DMA]
    rhs, scale = dual_rhs[0, 0], scaling[0, 0]
    direction = scale * rhs
    pack, report, corner_rows, facts = call(
        setup_kernel,
        "setup",
        [
            (slots * rows + 16, width),
            (corners + 8, LANES),
            (LANES, LANES),
            facts_shape,
        ],
        [
            pltpu.VMEM((slots, rows, width), BF16),
            pltpu.VMEM((slots, corners, rows), BF16),
            (slots, width),
            pltpu.VMEM((slots, corners), jnp.int32),
            pltpu.VMEM((slots, per), jnp.int32),
            pltpu.SMEM((1, 1), jnp.int32),
            (8, LANES),
            pltpu.SemaphoreType.DMA((6,)),
        ],
        [],
        [
            panel[0, 0],
            corner_panel[0, 0],
            interface_diag[0, 0],
            corner_map[0, 0],
            block_map[0, 0],
            counts,
        ],
        space=pltpu.HBM,
    )
    last = rhs
    directions, images, sums = [], [], []
    packs, late = [pack], []
    for sweep in range(3):
        partial = sweep == 1
        halo = [moved(direction, "gx", -1), moved(direction, "gx", 1)]
        if not partial:
            halo += [moved(direction, "gy", -1), moved(direction, "gy", 1)]
        extra = late if sweep else [report]
        size = 4 * owned + (0 if sweep else report.shape[0])
        groups = 3 if partial else 1
        (pay,) = call(
            functools.partial(before_kernel, slots, corners, per, sweep, groups, len(halo)),
            "before",
            [(size, LANES)],
            [(5 * groups * owned, block_size), (8, width), *facts_scratch],
            [],
            [
                direction,
                last,
                corner_rows,
                facts3 if partial else facts,
                *packs[:groups],
                *halo,
                *extra,
            ],
        )
        gathered = lax.all_gather(pay, "gy")
        if not sweep:
            gathered, leaving = lax.optimization_barrier((gathered, pack))
            packs = [pack, moved(leaving, "gy", -1), moved(leaving, "gy", 1)]
            here = y.reshape(1).astype(jnp.int32)
            inverse, place_rows, places3, facts3 = call(
                functools.partial(coarse_kernel, slots, corners, 4 * owned),
                "coarse",
                [(n, n), (peers, LANES), (3 * total, LANES), facts_shape],
                [(peers * total, n), (peers * total, n)],
                [here],
                [gathered, coarse_diag],
            )
        mine, east, west, sums, *late = call(
            functools.partial(after_kernel, slots, corners, per, sweep, partial),
            "after",
            [tile] * 3 + [(1, LANES)] * (2 if partial else 1),
            [(15 * owned, block_size), (8, width), (15 * owned, block_size), *facts_scratch],
            [here],
            [gathered, place_rows, places3, facts3, inverse, *packs, *([sums] if sweep else [])],
        )
        arrived = [moved(east, "gx", 1), moved(west, "gx", -1)]
        directions.append(direction)
        if sweep < 2:
            image = mine + arrived[0] + arrived[1]
            images.append(image)
            last, direction = image, STEP * scale * image
    across = lax.axis_size("gx")
    for group in (runs(across, 4), strided(across, 4)):
        sums = lax.all_gather(sums, "gx", axis=0, tiled=True, axis_index_groups=group)
        sums = jnp.sum(sums, axis=0, keepdims=True)
    multipliers, residual = call(
        functools.partial(final_kernel, total),
        "final",
        [tile] * 2,
        [],
        [],
        [sums, rhs, *directions, *images, mine, *arrived],
    )
    return multipliers[None, None], residual[None, None]


def solution(mesh):
    return jax.shard_map(
        shards,
        mesh=mesh,
        in_specs=(
            P("gx", "gy", None, None, None),
            P("gx", "gy", None, None, None),
            P("gx", "gy", None, None),
            P("gx", None),
            P("gx", "gy", None, None),
            P("gx", "gy", None, None),
            P("gx", "gy", None, None),
            P("gx", "gy", None, None),
            P("gx", "gy"),
        ),
        out_specs=(P("gx", "gy", None, None), P("gx", "gy", None, None)),
        check_vma=False,
    )
```

```python
import functools

import jax
import jax.numpy as jnp
from jax import lax
from jax.experimental import pallas as pl
from jax.experimental.pallas import tpu as pltpu
from jax.sharding import PartitionSpec as P

F32 = jnp.float32
BF16 = jnp.bfloat16
STEP = 0.00390625
LANES = 128
PIVOTS = 4


def iota(shape, dim):
    return lax.broadcasted_iota(jnp.int32, shape, dim)


def high(a, b):
    return jnp.dot(a, b, precision=lax.Precision.HIGHEST, preferred_element_type=F32)


def thirds(x):
    first = x.astype(BF16).astype(F32)
    rest = x - first
    second = rest.astype(BF16).astype(F32)
    return first, second, rest - second


def stacked(row):
    first, second, third = thirds(row)
    at = iota((16, 1), 0)
    rows = jnp.where(at == 0, first, jnp.where(at == 1, second, jnp.where(at == 2, third, 0.0)))
    return rows.astype(BF16)


def row_times(row, matrix, dim):
    out = lax.dot_general(
        stacked(row), matrix, (((1,), (dim,)), ((), ())), preferred_element_type=F32
    )
    return jnp.sum(out[:8], axis=0, keepdims=True)


def exact_times(x, hot):
    return sum(jnp.dot(piece.astype(BF16), hot, preferred_element_type=F32) for piece in thirds(x))


def inverse2(a, b, c):
    r = 1.0 / (a * c - b * b)
    return c * r, -b * r, a * r


def pivot_inverse(e):
    p = inverse2(e(0, 0), e(0, 1), e(1, 1))
    b = [[e(0, 2), e(0, 3)], [e(1, 2), e(1, 3)]]
    u = [
        [p[0] * b[0][j] + p[1] * b[1][j] for j in (0, 1)],
        [p[1] * b[0][j] + p[2] * b[1][j] for j in (0, 1)],
    ]
    s = inverse2(
        e(2, 2) - (b[0][0] * u[0][0] + b[1][0] * u[1][0]),
        e(2, 3) - (b[0][0] * u[0][1] + b[1][0] * u[1][1]),
        e(3, 3) - (b[0][1] * u[0][1] + b[1][1] * u[1][1]),
    )
    x = [[u[i][0] * s[0] + u[i][1] * s[1], u[i][0] * s[1] + u[i][1] * s[2]] for i in (0, 1)]
    p00 = p[0] + x[0][0] * u[0][0] + x[0][1] * u[0][1]
    p01 = p[1] + x[0][0] * u[1][0] + x[0][1] * u[1][1]
    p11 = p[2] + x[1][0] * u[1][0] + x[1][1] * u[1][1]
    return [
        [p00, p01, -x[0][0], -x[0][1]],
        [p01, p11, -x[1][0], -x[1][1]],
        [-x[0][0], -x[1][0], s[0], s[1]],
        [-x[0][1], -x[1][1], s[1], s[2]],
    ]


def small_inverse(a, n):
    lane = iota((1, n), 1)
    at8 = iota((8, 1), 0)
    for k in range(0, n, PIVOTS):
        rows = [a[k + i : k + i + 1, :] for i in range(PIVOTS)]
        cols = [jnp.broadcast_to(a[:, k + i : k + i + 1], (n, n)) for i in range(PIVOTS)]
        w = pivot_inverse(lambda i, j: cols[j][k + i : k + i + 1, :])
        inside = (lane >= k) & (lane < k + PIVOTS)
        units = [
            jnp.where(inside, jnp.where(lane == k + i, 1.0, 0.0), rows[i]) for i in range(PIVOTS)
        ]
        fresh = [sum(w[i][j] * units[j] for j in range(PIVOTS)) for i in range(PIVOTS)]
        base = jnp.where(inside, 0.0, a)
        for i in range(PIVOTS):
            base = base - cols[i] * fresh[i]
        v = k // 8 * 8
        block = base[v : v + 8]
        for i in range(PIVOTS):
            block = jnp.where(at8 == k + i - v, fresh[i], block)
        a = jnp.concatenate([x for x in (base[:v], block, base[v + 8 :]) if x.shape[0]], axis=0)
    return a


def setup_kernel(
    panel_hbm, corner_hbm, diag_hbm, place_hbm, map_hbm, count_hbm, pack_ref, report_ref, rows_ref, facts_ref, panel_ref, corner_ref, diag_ref,
    place_ref, map_ref, count_ref, facts, sems,
):
    slots, rows, width = panel_ref.shape
    corners = corner_ref.shape[1]
    per = map_ref.shape[1]
    total = slots * corners
    at = slots * rows
    moves = (
        (corner_hbm, corner_ref),
        (place_hbm, place_ref),
        (map_hbm, map_ref),
        (count_hbm, count_ref),
        (diag_hbm, diag_ref),
        (panel_hbm, panel_ref),
    )
    copies = [pltpu.make_async_copy(a, b, sems.at[i]) for i, (a, b) in enumerate(moves)]
    for copy in copies:
        copy.start()
    pack_ref[at:, :] = jnp.zeros((16, width), F32)
    rows_ref[...] = jnp.zeros_like(rows_ref)
    facts[...] = jnp.zeros_like(facts)
    for copy in copies:
        copy.wait()
    pack_ref[at + 8 : at + 8 + slots, :] = diag_ref[...]
    lane = iota((1, LANES), 1)
    for s in range(slots):
        pack_ref[s * rows : (s + 1) * rows, :] = panel_ref[s].astype(F32)
        rows_ref[s * corners : (s + 1) * corners, :] = corner_ref[s].astype(F32)
        facts[s : s + 1, :corners] = place_ref[s : s + 1, :].astype(F32)
        facts[slots + s : slots + s + 1, :per] = map_ref[s : s + 1, :].astype(F32)
    for i in range(total // 8):
        pack_ref[at : at + 8, i * LANES : (i + 1) * LANES] = rows_ref[8 * i : 8 * i + 8, :]
    narrow = rows_ref[...].astype(BF16)
    square = lax.dot_general(
        narrow, narrow, (((1,), (1,)), ((), ())), preferred_element_type=F32
    )
    part = jnp.zeros((corners, LANES), F32)
    count = count_ref[0, 0]
    fact = jnp.where(lane == total + slots * per, count.astype(F32), 0.0)
    for s in range(slots):
        live = jnp.where(s < count, 1.0, 0.0)
        first = s * corners
        mine = (lane >= first) & (lane < first + corners)
        part = jnp.where(mine, square[first : first + corners, :] * live, part)
        row = facts[s : s + 1, :]
        column = jnp.sum(
            jnp.where(iota((corners, 1), 0) == lane, row, 0.0), axis=1, keepdims=True
        )
        part = jnp.where(lane == total + s, column, part)
        fact = fact + (pltpu.roll(row, first, 1) if s else row)
        fact = fact + pltpu.roll(facts[slots + s : slots + s + 1, :], total + s * per, 1)
    report_ref[:corners, :] = part
    report_ref[corners:, :] = jnp.broadcast_to(fact, (8, LANES))
    facts_ref[...] = jnp.broadcast_to(fact.astype(jnp.int32), (8, LANES))


def flipped(a, b):
    return lax.dot_general(
        a, b, (((1,), (1,)), ((), ())), precision=lax.Precision.HIGHEST, preferred_element_type=F32
    )


def split_inverse(m, n):
    h = n // 2
    a, b, bt, c = m[:h, :h], m[:h, h:], m[h:, :h], m[h:, h:]
    ai = small_inverse(a, h)
    u = high(ai, b)
    si = small_inverse(c - high(bt, u), h)
    x, xt = high(u, si), flipped(si, u)
    top = jnp.concatenate([ai + flipped(x, u), -x], axis=1)
    return jnp.concatenate([top, jnp.concatenate([-xt, si], axis=1)], axis=0)


def coarse_kernel(
    slots, corners, start, y_ref, gathered_ref, diag_ref, out_ref, rows_ref, places_ref, facts_ref,
    hot_ref, spread_ref,
):
    count = gathered_ref.shape[0]
    total = slots * corners
    n = diag_ref.shape[1]
    lane = iota((1, n), 1).astype(F32)
    for y in range(count):
        part = gathered_ref[y, start : start + corners, :]
        rows_ref[y : y + 1, :] = gathered_ref[y, start + corners : start + corners + 1, :]
        for s in range(slots):
            block = part[:, s * corners : (s + 1) * corners]
            place = part[:, total + s : total + s + 1]
            hot = jnp.where(place == lane, 1.0, 0.0)
            at = (y * slots + s) * corners
            hot_ref[at : at + corners, :] = hot
            spread_ref[at : at + corners, :] = exact_times(block, hot.astype(BF16))
    facts_ref[...] = jnp.zeros_like(facts_ref)
    for g, by in enumerate((0, 1, -1)):
        there = y_ref[0] + by
        y = jnp.clip(there, 0, count - 1)
        fact = gathered_ref[y, start + corners : start + corners + 1, :].astype(jnp.int32)
        facts_ref[g : g + 1, :] = jnp.where((there >= 0) & (there < count), fact, 0)
        part = gathered_ref[y, start : start + corners, :]
        for s in range(slots):
            at = g * total + s * corners
            places_ref[at : at + corners, :] = jnp.broadcast_to(
                part[:, total + s : total + s + 1], (corners, LANES)
            )
    hots = hot_ref[...].astype(BF16)
    system = jnp.where(iota((n, 1), 0) == iota((1, n), 1), diag_ref[...], 0.0)
    for piece in thirds(spread_ref[...]):
        system = system + lax.dot_general(
            hots, piece.astype(BF16), (((0,), (0,)), ((), ())), preferred_element_type=F32
        )
    out_ref[...] = system
    eliminated(out_ref, 0, 1)


def rest_kernel(system_ref, out_ref):
    out_ref[...] = system_ref[...]
    eliminated(out_ref, 1, out_ref.shape[0] // LANES)


def eliminated(out_ref, first, last):
    n = out_ref.shape[0]
    b = LANES

    def eliminate(k, carry):
        ro = pl.multiple_of(k * b, b)
        pivots = split_inverse(out_ref[pl.ds(ro, b), pl.ds(ro, b)], b)
        col = out_ref[:, pl.ds(ro, b)]
        out_ref[:, pl.ds(ro, b)] = jnp.zeros((n, b), F32)
        out_ref[pl.ds(ro, b), pl.ds(ro, b)] = jnp.where(iota((b, b), 0) == iota((b, b), 1), 1.0, 0.0)
        fresh = high(pivots, out_ref[pl.ds(ro, b), :])
        out_ref[pl.ds(ro, b), :] = jnp.zeros((b, n), F32)
        at = iota((n, 1), 0)
        others = jnp.where((at >= ro) & (at < ro + b), 0.0, col)
        out_ref[...] = out_ref[...] - high(others, fresh)
        out_ref[pl.ds(ro, b), :] = fresh
        return carry

    lax.fori_loop(first, last, eliminate, 0)


def fact_of(facts, slots, corners, per, g, s, b, owned):
    k = facts[g, slots * corners + s * per + b]
    live = jnp.where(s < facts[g, slots * corners + slots * per], 1.0, 0.0)
    return k, jnp.where(k < owned, live, -live)


def gathered_rows(slots, corners, per, owned, g, facts, cand, u_ref):
    for s in range(slots):
        for b in range(per):
            k, sign = fact_of(facts, slots, corners, per, g, s, b, owned)
            row = cand[pl.ds(g * 5 * owned + k, 1), :] * sign
            u_ref[g * slots + s : g * slots + s + 1, b * LANES : (b + 1) * LANES] = row


def before_kernel(slots, corners, per, sweep, groups, parts, v_ref, last_ref, corner_ref, facts_ref, *rest):
    rest, (pay_ref, cand, u_ref, facts, sem) = rest[:-5], rest[-5:]
    packs, halo, extra = rest[:groups], rest[groups : groups + parts], rest[groups + parts :]
    copy = pltpu.make_async_copy(facts_ref, facts, sem)
    copy.start()
    owned = v_ref.shape[0]
    total = slots * corners
    v = v_ref[...]
    if groups > 1:
        cand[...] = jnp.zeros_like(cand)
        cand[9 * owned : 10 * owned, :] = v
        cand[13 * owned : 14 * owned, :] = v
    for i, ref in enumerate((v_ref, *halo)):
        cand[i * owned : (i + 1) * owned, :] = ref[...]
        if i < 3:
            pay_ref[i * owned : (i + 1) * owned, :] = ref[...]
    at = iota((owned, 1), 0)
    lane = iota((1, LANES), 1)
    energy = jnp.sum(v * v, keepdims=True)
    pays = []
    copy.wait()
    for g in range(groups):
        pack = packs[g]
        rows = (pack.shape[0] - 16) // slots
        pay = jnp.zeros((1, LANES), F32)
        gathered_rows(slots, corners, per, owned, g, facts, cand, u_ref)
        for s in range(slots):
            live = jnp.where(s < facts[g, total + slots * per], 1.0, 0.0)
            u = u_ref[g * slots + s : g * slots + s + 1, :]
            t = row_times(u, pack[s * rows : (s + 1) * rows, :].astype(BF16), 1)
            energy = energy + jnp.sum(t * t, keepdims=True)
            weights = pack[slots * rows + 8 + s : slots * rows + 9 + s, :]
            energy = energy + jnp.sum(weights * u * u, keepdims=True)
            first = s * corners
            if g:
                j = slots * rows
                narrow = [
                    pack[j : j + 8, i * LANES : (i + 1) * LANES] for i in range(total // 8)
                ]
                narrow = jnp.concatenate(narrow + [jnp.zeros((LANES - total, LANES), F32)], axis=0)
            else:
                narrow = corner_ref[...]
            c = row_times(t, narrow.astype(BF16), 1) * live
            pay = jnp.where((lane >= first) & (lane < first + corners), c, pay)
        pays.append(pay)
    cross = jnp.sum(v * last_ref[...], keepdims=True)
    pay = pays[0]
    if groups == 1:
        pay = jnp.where(lane == total + 2 * sweep, energy, pay)
    pay = jnp.where(lane == total + 2 * sweep + 1, cross, pay)
    for ref in extra:
        if ref.shape[0] == 1:
            pay = pay + ref[...]
        else:
            pay_ref[4 * owned :, :] = ref[...]
    block = jnp.where(at == 0, pay, 0.0)
    for g in range(1, groups):
        block = jnp.where(at == g, pays[g], block)
    pay_ref[3 * owned : 4 * owned, :] = block


def after_kernel(
    slots, corners, per, sweep, partial, y_ref, gathered_ref, rows_ref, places_ref, facts_ref, inverse_ref,
    *rest,
):
    packs, rest = rest[:3], rest[3:]
    before, rest = rest[: 1 if sweep else 0], rest[1 if sweep else 0 :]
    late, (cand, u_ref, acc, facts, sem) = rest[4:-5], rest[-5:]
    mine, east, west, sums_ref = rest[:4]
    copy = pltpu.make_async_copy(facts_ref, facts, sem)
    copy.start()
    owned = mine.shape[0]
    total = slots * corners
    n = inverse_ref.shape[0]
    count = gathered_ref.shape[0]
    middle = y_ref[0]
    field = {}
    for by in (0, 1, -1, 2, -2):
        y = middle + by
        inside = jnp.where((y >= 0) & (y < count), 1.0, 0.0)
        p = jnp.clip(y, 0, count - 1)
        for i in range(3 if abs(by) < 2 else 1):
            field[by, i] = gathered_ref[p, i * owned : (i + 1) * owned, :] * inside
    for g, by in enumerate((0, 1, -1)):
        parts = (field[by, 0], field[by, 1], field[by, 2])
        parts += (field[by + 1, 0] if by < 2 else None, field[by - 1, 0])
        for i, part in enumerate(parts):
            at = (5 * g + i) * owned
            cand[at : at + owned, :] = part
    lane = iota((1, LANES), 1)
    at = iota((n, 1), 0)
    spread = jnp.zeros((n, LANES), F32)
    totals = jnp.zeros((1, LANES), F32)
    places = rows_ref[...].astype(jnp.int32)
    for p in range(count):
        row = gathered_ref[p, 3 * owned : 3 * owned + 1, :]
        if partial and p > 0:
            row = row + gathered_ref[p - 1, 3 * owned + 1 : 3 * owned + 2, :]
        if partial and p < count - 1:
            row = row + gathered_ref[p + 1, 3 * owned + 2 : 3 * owned + 3, :]
        totals = totals + row
        spread = spread + jnp.where(places[p : p + 1, :] == at, row, 0.0)
    right = jnp.sum(jnp.where(lane < total, spread, 0.0), axis=1, keepdims=True)
    coarse = jnp.sum(inverse_ref[...] * right, axis=0, keepdims=True)
    wide = iota((1, n), 1)
    right_row = jnp.sum(jnp.where(at == wide, right, 0.0), axis=0, keepdims=True)
    energy = jnp.sum(coarse * right_row, keepdims=True)
    totals = totals + jnp.where(lane == total + 2 * sweep, energy, 0.0)
    for ref in before:
        totals = totals + ref[...]
    sums_ref[...] = totals
    acc[...] = jnp.zeros_like(acc)
    acc[:owned, :] = field[0, 0]
    copy.wait()
    for g in range(3):
        gathered_rows(slots, corners, per, owned, g, facts, cand, u_ref)
    wide = wide.astype(F32)
    local = jnp.sum(field[0, 0] * field[0, 0], keepdims=True)
    for g in range(3):
        pack = packs[g]
        rows = (pack.shape[0] - 16) // slots
        tail = slots * rows
        for s in range(slots):
            panel = pack[s * rows : (s + 1) * rows, :].astype(BF16)
            u = u_ref[g * slots + s : g * slots + s + 1, :]
            t = row_times(u, panel, 1)
            weights = pack[tail + 8 + s : tail + 9 + s, :]
            if g == 0:
                local = local + jnp.sum(t * t, keepdims=True)
                local = local + jnp.sum(weights * u * u, keepdims=True)
            for i in range(corners // 8):
                first = s * corners + 8 * i
                place = places_ref[g * total + first : g * total + first + 8, :1]
                back = jnp.sum(jnp.where(place == wide, coarse, 0.0), axis=1, keepdims=True)
                j = first // 8
                part = pack[tail : tail + 8, j * LANES : (j + 1) * LANES]
                t = t + jnp.sum(back * part, axis=0, keepdims=True)
            w = row_times(t, panel, 0) + weights * u
            for b in range(per):
                k, sign = fact_of(facts, slots, corners, per, g, s, b, owned)
                acc[pl.ds(g * 5 * owned + k, 1), :] += w[:, b * LANES : (b + 1) * LANES] * sign
    mine[...] = acc[:owned, :] + acc[9 * owned : 10 * owned, :] + acc[13 * owned : 14 * owned, :]
    for ref in late:
        ref[...] = jnp.where(lane == total + 2 * sweep, local, 0.0)
    east[...] = acc[owned : 2 * owned, :]
    west[...] = acc[2 * owned : 3 * owned, :]


def final_kernel(first, gathered_ref, rhs_ref, v0, v1, v2, w0, w1, mine, east, west, x_ref, r_ref):
    sums = gathered_ref[...]
    lane = iota((1, LANES), 1)

    def moment(i):
        return jnp.sum(jnp.where(lane == first + i, sums, 0.0), axis=1, keepdims=True)

    h00, r0, h11, h01, h22, h12 = (moment(i) for i in range(6))
    h02, r1, r2 = h11, STEP * h00, STEP * h01
    l10, l20 = h01 / h00, h02 / h00
    d1 = h11 - l10 * h01
    e12 = h12 - l10 * h02
    l21 = e12 / d1
    d2 = h22 - l20 * h02 - l21 * e12
    y1 = r1 - l10 * r0
    y2 = r2 - l20 * r0 - l21 * y1
    c2 = y2 / d2
    c1 = y1 / d1 - l21 * c2
    c0 = r0 / h00 - l10 * c1 - l20 * c2
    w2 = mine[...] + east[...] + west[...]
    x_ref[...] = c0 * v0[...] + c1 * v1[...] + c2 * v2[...]
    r_ref[...] = rhs_ref[...] - (c0 * w0[...] + c1 * w1[...] + c2 * w2)


def call(kernel, name, outs, scratch, scalars, arrays, space=pltpu.VMEM):
    vmem = pl.BlockSpec(memory_space=pltpu.VMEM)
    smem = pl.BlockSpec(memory_space=pltpu.SMEM)
    outs = [x if isinstance(x, jax.ShapeDtypeStruct) else jax.ShapeDtypeStruct(x, F32) for x in outs]
    return pl.pallas_call(
        kernel,
        out_shape=outs,
        in_specs=[smem] * len(scalars) + [pl.BlockSpec(memory_space=space)] * len(arrays),
        out_specs=[vmem] * len(outs),
        scratch_shapes=[pltpu.VMEM(x, F32) if isinstance(x, tuple) else x for x in scratch],
        compiler_params=pltpu.CompilerParams(vmem_limit_bytes=40 << 20),
        name=name,
    )(*scalars, *arrays)


def moved(x, axis, by):
    count = lax.axis_size(axis)
    return lax.ppermute(x, axis, [(i, i + by) for i in range(count) if 0 <= i + by < count])


def strided(count, by):
    return [list(range(i, count, by)) for i in range(by)]


def runs(count, size):
    return [list(range(i, i + size)) for i in range(0, count, size)]


def shards(
    panel, corner_panel, interface_diag, coarse_diag, scaling, dual_rhs, block_map, corner_map, counts
):
    slots, rows, width = panel.shape[2:]
    corners = corner_panel.shape[3]
    owned, block_size = scaling.shape[2:]
    n = coarse_diag.shape[1]
    total = slots * corners
    peers = lax.axis_size("gy")
    y = lax.axis_index("gy")
    per = block_map.shape[3]
    tile = (owned, block_size)
    facts_shape = jax.ShapeDtypeStruct((8, LANES), jnp.int32)
    facts_scratch = [pltpu.SMEM((8, LANES), jnp.int32), pltpu.SemaphoreType.DMA]
    rhs, scale = dual_rhs[0, 0], scaling[0, 0]
    direction = scale * rhs
    pack, report, corner_rows, facts = call(
        setup_kernel,
        "setup",
        [
            (slots * rows + 16, width),
            (corners + 8, LANES),
            (LANES, LANES),
            facts_shape,
        ],
        [
            pltpu.VMEM((slots, rows, width), BF16),
            pltpu.VMEM((slots, corners, rows), BF16),
            (slots, width),
            pltpu.VMEM((slots, corners), jnp.int32),
            pltpu.VMEM((slots, per), jnp.int32),
            pltpu.SMEM((1, 1), jnp.int32),
            (8, LANES),
            pltpu.SemaphoreType.DMA((6,)),
        ],
        [],
        [
            panel[0, 0],
            corner_panel[0, 0],
            interface_diag[0, 0],
            corner_map[0, 0],
            block_map[0, 0],
            counts,
        ],
        space=pltpu.HBM,
    )
    last = rhs
    directions, images, sums = [], [], []
    packs, late = [pack], []
    for sweep in range(3):
        partial = sweep == 1
        halo = [moved(direction, "gx", -1), moved(direction, "gx", 1)]
        if not partial:
            halo += [moved(direction, "gy", -1), moved(direction, "gy", 1)]
        extra = late if sweep else [report]
        size = 4 * owned + (0 if sweep else report.shape[0])
        groups = 3 if partial else 1
        (pay,) = call(
            functools.partial(before_kernel, slots, corners, per, sweep, groups, len(halo)),
            "before",
            [(size, LANES)],
            [(5 * groups * owned, block_size), (8, width), *facts_scratch],
            [],
            [
                direction,
                last,
                corner_rows,
                facts3 if partial else facts,
                *packs[:groups],
                *halo,
                *extra,
            ],
        )
        gathered = lax.all_gather(pay, "gy")
        if not sweep:
            here = y.reshape(1).astype(jnp.int32)
            started, place_rows, places3, facts3 = call(
                functools.partial(coarse_kernel, slots, corners, 4 * owned),
                "coarse",
                [(n, n), (peers, LANES), (3 * total, LANES), facts_shape],
                [(peers * total, n), (peers * total, n)],
                [here],
                [gathered, coarse_diag],
            )
            started, leaving = lax.optimization_barrier((started, pack))
            packs = [pack, moved(leaving, "gy", -1), moved(leaving, "gy", 1)]
            (inverse,) = call(rest_kernel, "rest", [(n, n)], [], [], [started])
        mine, east, west, sums, *late = call(
            functools.partial(after_kernel, slots, corners, per, sweep, partial),
            "after",
            [tile] * 3 + [(1, LANES)] * (2 if partial else 1),
            [(15 * owned, block_size), (8, width), (15 * owned, block_size), *facts_scratch],
            [here],
            [gathered, place_rows, places3, facts3, inverse, *packs, *([sums] if sweep else [])],
        )
        arrived = [moved(east, "gx", 1), moved(west, "gx", -1)]
        directions.append(direction)
        if sweep < 2:
            image = mine + arrived[0] + arrived[1]
            images.append(image)
            last, direction = image, STEP * scale * image
    across = lax.axis_size("gx")
    for group in (runs(across, 4), strided(across, 4)):
        sums = lax.all_gather(sums, "gx", axis=0, tiled=True, axis_index_groups=group)
        sums = jnp.sum(sums, axis=0, keepdims=True)
    multipliers, residual = call(
        functools.partial(final_kernel, total),
        "final",
        [tile] * 2,
        [],
        [],
        [sums, rhs, *directions, *images, mine, *arrived],
    )
    return multipliers[None, None], residual[None, None]


def solution(mesh):
    return jax.shard_map(
        shards,
        mesh=mesh,
        in_specs=(
            P("gx", "gy", None, None, None),
            P("gx", "gy", None, None, None),
            P("gx", "gy", None, None),
            P("gx", None),
            P("gx", "gy", None, None),
            P("gx", "gy", None, None),
            P("gx", "gy", None, None),
            P("gx", "gy", None, None),
            P("gx", "gy"),
        ),
        out_specs=(P("gx", "gy", None, None), P("gx", "gy", None, None)),
        check_vma=False,
    )
```

```python
import functools

import jax
import jax.numpy as jnp
from jax import lax
from jax.experimental import pallas as pl
from jax.experimental.pallas import tpu as pltpu
from jax.sharding import PartitionSpec as P

F32 = jnp.float32
BF16 = jnp.bfloat16
STEP = 0.00390625
LANES = 128
PIVOTS = 4


def iota(shape, dim):
    return lax.broadcasted_iota(jnp.int32, shape, dim)


def high(a, b):
    return jnp.dot(a, b, precision=lax.Precision.HIGHEST, preferred_element_type=F32)


def thirds(x):
    first = x.astype(BF16).astype(F32)
    rest = x - first
    second = rest.astype(BF16).astype(F32)
    return first, second, rest - second


def stacked(row):
    first, second, third = thirds(row)
    at = iota((16, 1), 0)
    rows = jnp.where(at == 0, first, jnp.where(at == 1, second, jnp.where(at == 2, third, 0.0)))
    return rows.astype(BF16)


def row_times(row, matrix, dim):
    out = lax.dot_general(
        stacked(row), matrix, (((1,), (dim,)), ((), ())), preferred_element_type=F32
    )
    return jnp.sum(out[:8], axis=0, keepdims=True)


def exact_times(x, hot):
    return sum(jnp.dot(piece.astype(BF16), hot, preferred_element_type=F32) for piece in thirds(x))


def inverse2(a, b, c):
    r = 1.0 / (a * c - b * b)
    return c * r, -b * r, a * r


def pivot_inverse(e):
    p = inverse2(e(0, 0), e(0, 1), e(1, 1))
    b = [[e(0, 2), e(0, 3)], [e(1, 2), e(1, 3)]]
    u = [
        [p[0] * b[0][j] + p[1] * b[1][j] for j in (0, 1)],
        [p[1] * b[0][j] + p[2] * b[1][j] for j in (0, 1)],
    ]
    s = inverse2(
        e(2, 2) - (b[0][0] * u[0][0] + b[1][0] * u[1][0]),
        e(2, 3) - (b[0][0] * u[0][1] + b[1][0] * u[1][1]),
        e(3, 3) - (b[0][1] * u[0][1] + b[1][1] * u[1][1]),
    )
    x = [[u[i][0] * s[0] + u[i][1] * s[1], u[i][0] * s[1] + u[i][1] * s[2]] for i in (0, 1)]
    p00 = p[0] + x[0][0] * u[0][0] + x[0][1] * u[0][1]
    p01 = p[1] + x[0][0] * u[1][0] + x[0][1] * u[1][1]
    p11 = p[2] + x[1][0] * u[1][0] + x[1][1] * u[1][1]
    return [
        [p00, p01, -x[0][0], -x[0][1]],
        [p01, p11, -x[1][0], -x[1][1]],
        [-x[0][0], -x[1][0], s[0], s[1]],
        [-x[0][1], -x[1][1], s[1], s[2]],
    ]


def small_inverse(a, n):
    lane = iota((1, n), 1)
    at8 = iota((8, 1), 0)
    for k in range(0, n, PIVOTS):
        rows = [a[k + i : k + i + 1, :] for i in range(PIVOTS)]
        cols = [jnp.broadcast_to(a[:, k + i : k + i + 1], (n, n)) for i in range(PIVOTS)]
        w = pivot_inverse(lambda i, j: cols[j][k + i : k + i + 1, :])
        inside = (lane >= k) & (lane < k + PIVOTS)
        units = [
            jnp.where(inside, jnp.where(lane == k + i, 1.0, 0.0), rows[i]) for i in range(PIVOTS)
        ]
        fresh = [sum(w[i][j] * units[j] for j in range(PIVOTS)) for i in range(PIVOTS)]
        base = jnp.where(inside, 0.0, a)
        for i in range(PIVOTS):
            base = base - cols[i] * fresh[i]
        v = k // 8 * 8
        block = base[v : v + 8]
        for i in range(PIVOTS):
            block = jnp.where(at8 == k + i - v, fresh[i], block)
        a = jnp.concatenate([x for x in (base[:v], block, base[v + 8 :]) if x.shape[0]], axis=0)
    return a


def setup_kernel(
    panel_hbm, corner_hbm, diag_hbm, place_hbm, map_hbm, count_hbm, pack_ref, report_ref, rows_ref, facts_ref, panel_ref, corner_ref, diag_ref,
    place_ref, map_ref, count_ref, facts, sems,
):
    slots, rows, width = panel_ref.shape
    corners = corner_ref.shape[1]
    per = map_ref.shape[1]
    total = slots * corners
    at = slots * rows
    moves = (
        (corner_hbm, corner_ref),
        (place_hbm, place_ref),
        (map_hbm, map_ref),
        (count_hbm, count_ref),
        (diag_hbm, diag_ref),
        (panel_hbm, panel_ref),
    )
    copies = [pltpu.make_async_copy(a, b, sems.at[i]) for i, (a, b) in enumerate(moves)]
    for copy in copies:
        copy.start()
    pack_ref[at:, :] = jnp.zeros((16, width), F32)
    rows_ref[...] = jnp.zeros_like(rows_ref)
    facts[...] = jnp.zeros_like(facts)
    for copy in copies:
        copy.wait()
    pack_ref[at + 8 : at + 8 + slots, :] = diag_ref[...]
    lane = iota((1, LANES), 1)
    for s in range(slots):
        pack_ref[s * rows : (s + 1) * rows, :] = panel_ref[s].astype(F32)
        rows_ref[s * corners : (s + 1) * corners, :] = corner_ref[s].astype(F32)
        facts[s : s + 1, :corners] = place_ref[s : s + 1, :].astype(F32)
        facts[slots + s : slots + s + 1, :per] = map_ref[s : s + 1, :].astype(F32)
    for i in range(total // 8):
        pack_ref[at : at + 8, i * LANES : (i + 1) * LANES] = rows_ref[8 * i : 8 * i + 8, :]
    narrow = rows_ref[...].astype(BF16)
    square = lax.dot_general(
        narrow, narrow, (((1,), (1,)), ((), ())), preferred_element_type=F32
    )
    part = jnp.zeros((corners, LANES), F32)
    count = count_ref[0, 0]
    fact = jnp.where(lane == total + slots * per, count.astype(F32), 0.0)
    for s in range(slots):
        live = jnp.where(s < count, 1.0, 0.0)
        first = s * corners
        mine = (lane >= first) & (lane < first + corners)
        part = jnp.where(mine, square[first : first + corners, :] * live, part)
        row = facts[s : s + 1, :]
        column = jnp.sum(
            jnp.where(iota((corners, 1), 0) == lane, row, 0.0), axis=1, keepdims=True
        )
        part = jnp.where(lane == total + s, column, part)
        fact = fact + (pltpu.roll(row, first, 1) if s else row)
        fact = fact + pltpu.roll(facts[slots + s : slots + s + 1, :], total + s * per, 1)
    report_ref[:corners, :] = part
    report_ref[corners:, :] = jnp.broadcast_to(fact, (8, LANES))
    facts_ref[...] = jnp.broadcast_to(fact.astype(jnp.int32), (8, LANES))


def flipped(a, b):
    return lax.dot_general(
        a, b, (((1,), (1,)), ((), ())), precision=lax.Precision.HIGHEST, preferred_element_type=F32
    )


def split_inverse(m, n):
    h = n // 2
    a, b, bt, c = m[:h, :h], m[:h, h:], m[h:, :h], m[h:, h:]
    ai = small_inverse(a, h)
    u = high(ai, b)
    si = small_inverse(c - high(bt, u), h)
    x, xt = high(u, si), flipped(si, u)
    top = jnp.concatenate([ai + flipped(x, u), -x], axis=1)
    return jnp.concatenate([top, jnp.concatenate([-xt, si], axis=1)], axis=0)


def coarse_kernel(
    slots, corners, start, y_ref, gathered_ref, diag_ref, out_ref, rows_ref, places_ref, facts_ref,
    hot_ref, spread_ref,
):
    count = gathered_ref.shape[0]
    total = slots * corners
    n = diag_ref.shape[1]
    lane = iota((1, n), 1).astype(F32)
    for y in range(count):
        part = gathered_ref[y, start : start + corners, :]
        rows_ref[y : y + 1, :] = gathered_ref[y, start + corners : start + corners + 1, :]
        for s in range(slots):
            block = part[:, s * corners : (s + 1) * corners]
            place = part[:, total + s : total + s + 1]
            hot = jnp.where(place == lane, 1.0, 0.0)
            at = (y * slots + s) * corners
            hot_ref[at : at + corners, :] = hot
            spread_ref[at : at + corners, :] = exact_times(block, hot.astype(BF16))
    facts_ref[...] = jnp.zeros_like(facts_ref)
    for g, by in enumerate((0, 1, -1)):
        there = y_ref[0] + by
        y = jnp.clip(there, 0, count - 1)
        fact = gathered_ref[y, start + corners : start + corners + 1, :].astype(jnp.int32)
        facts_ref[g : g + 1, :] = jnp.where((there >= 0) & (there < count), fact, 0)
        part = gathered_ref[y, start : start + corners, :]
        for s in range(slots):
            at = g * total + s * corners
            places_ref[at : at + corners, :] = jnp.broadcast_to(
                part[:, total + s : total + s + 1], (corners, LANES)
            )
    hots = hot_ref[...].astype(BF16)
    system = jnp.where(iota((n, 1), 0) == iota((1, n), 1), diag_ref[...], 0.0)
    for piece in thirds(spread_ref[...]):
        system = system + lax.dot_general(
            hots, piece.astype(BF16), (((0,), (0,)), ((), ())), preferred_element_type=F32
        )
    out_ref[...] = system
    eliminated(out_ref, 0, 1)


def rest_kernel(system_ref, out_ref):
    out_ref[...] = system_ref[...]
    eliminated(out_ref, 1, out_ref.shape[0] // LANES)


def eliminated(out_ref, first, last):
    n = out_ref.shape[0]
    b = LANES

    def eliminate(k, carry):
        ro = pl.multiple_of(k * b, b)
        pivots = split_inverse(out_ref[pl.ds(ro, b), pl.ds(ro, b)], b)
        col = out_ref[:, pl.ds(ro, b)]
        out_ref[:, pl.ds(ro, b)] = jnp.zeros((n, b), F32)
        out_ref[pl.ds(ro, b), pl.ds(ro, b)] = jnp.where(iota((b, b), 0) == iota((b, b), 1), 1.0, 0.0)
        fresh = high(pivots, out_ref[pl.ds(ro, b), :])
        out_ref[pl.ds(ro, b), :] = jnp.zeros((b, n), F32)
        at = iota((n, 1), 0)
        others = jnp.where((at >= ro) & (at < ro + b), 0.0, col)
        out_ref[...] = out_ref[...] - high(others, fresh)
        out_ref[pl.ds(ro, b), :] = fresh
        return carry

    lax.fori_loop(first, last, eliminate, 0)


def fact_of(facts, slots, corners, per, g, s, b, owned):
    k = facts[g, slots * corners + s * per + b]
    live = jnp.where(s < facts[g, slots * corners + slots * per], 1.0, 0.0)
    return k, jnp.where(k < owned, live, -live)


def gathered_rows(slots, corners, per, owned, g, facts, cand, u_ref):
    for s in range(slots):
        for b in range(per):
            k, sign = fact_of(facts, slots, corners, per, g, s, b, owned)
            row = cand[pl.ds(g * 5 * owned + k, 1), :] * sign
            u_ref[g * slots + s : g * slots + s + 1, b * LANES : (b + 1) * LANES] = row


def before_kernel(slots, corners, per, sweep, groups, parts, v_ref, last_ref, corner_ref, facts_ref, *rest):
    rest, (pay_ref, cand, u_ref, facts, sem) = rest[:-5], rest[-5:]
    packs, halo, extra = rest[:groups], rest[groups : groups + parts], rest[groups + parts :]
    copy = pltpu.make_async_copy(facts_ref, facts, sem)
    copy.start()
    owned = v_ref.shape[0]
    total = slots * corners
    v = v_ref[...]
    if groups > 1:
        cand[...] = jnp.zeros_like(cand)
        cand[9 * owned : 10 * owned, :] = v
        cand[13 * owned : 14 * owned, :] = v
    for i, ref in enumerate((v_ref, *halo)):
        cand[i * owned : (i + 1) * owned, :] = ref[...]
        if i < 3:
            pay_ref[i * owned : (i + 1) * owned, :] = ref[...]
    at = iota((owned, 1), 0)
    lane = iota((1, LANES), 1)
    energy = jnp.sum(v * v, keepdims=True)
    pays = []
    copy.wait()
    for g in range(groups):
        pack = packs[g]
        rows = (pack.shape[0] - 16) // slots
        pay = jnp.zeros((1, LANES), F32)
        gathered_rows(slots, corners, per, owned, g, facts, cand, u_ref)
        for s in range(slots):
            live = jnp.where(s < facts[g, total + slots * per], 1.0, 0.0)
            u = u_ref[g * slots + s : g * slots + s + 1, :]
            t = row_times(u, pack[s * rows : (s + 1) * rows, :].astype(BF16), 1)
            energy = energy + jnp.sum(t * t, keepdims=True)
            weights = pack[slots * rows + 8 + s : slots * rows + 9 + s, :]
            energy = energy + jnp.sum(weights * u * u, keepdims=True)
            first = s * corners
            if g:
                j = slots * rows
                narrow = [
                    pack[j : j + 8, i * LANES : (i + 1) * LANES] for i in range(total // 8)
                ]
                narrow = jnp.concatenate(narrow + [jnp.zeros((LANES - total, LANES), F32)], axis=0)
            else:
                narrow = corner_ref[...]
            c = row_times(t, narrow.astype(BF16), 1) * live
            pay = jnp.where((lane >= first) & (lane < first + corners), c, pay)
        pays.append(pay)
    cross = jnp.sum(v * last_ref[...], keepdims=True)
    pay = pays[0]
    if groups == 1:
        pay = jnp.where(lane == total + 2 * sweep, energy, pay)
    pay = jnp.where(lane == total + 2 * sweep + 1, cross, pay)
    for ref in extra:
        if ref.shape[0] == 1:
            pay = pay + ref[...]
        else:
            pay_ref[4 * owned :, :] = ref[...]
    block = jnp.where(at == 0, pay, 0.0)
    for g in range(1, groups):
        block = jnp.where(at == g, pays[g], block)
    pay_ref[3 * owned : 4 * owned, :] = block


def after_kernel(
    slots, corners, per, sweep, partial, y_ref, gathered_ref, rows_ref, places_ref, facts_ref, inverse_ref,
    *rest,
):
    packs, rest = rest[:3], rest[3:]
    before, rest = rest[: 1 if sweep else 0], rest[1 if sweep else 0 :]
    outs, (cand, u_ref, acc, facts, sem) = rest[:-5], rest[-5:]
    last = len(outs) == 2
    mine, late = outs[0], outs[4:]
    owned = mine.shape[0]
    if last:
        sums_ref = outs[1].at[:1, :]
        east, west = outs[1].at[owned : 2 * owned, :], outs[1].at[2 * owned :, :]
        outs[1][:owned, :] = jnp.zeros((owned, LANES), F32)
    else:
        east, west, sums_ref = outs[1:4]
    copy = pltpu.make_async_copy(facts_ref, facts, sem)
    copy.start()
    total = slots * corners
    n = inverse_ref.shape[0]
    count = gathered_ref.shape[0]
    middle = y_ref[0]
    field = {}
    for by in (0, 1, -1, 2, -2):
        y = middle + by
        inside = jnp.where((y >= 0) & (y < count), 1.0, 0.0)
        p = jnp.clip(y, 0, count - 1)
        for i in range(3 if abs(by) < 2 else 1):
            field[by, i] = gathered_ref[p, i * owned : (i + 1) * owned, :] * inside
    for g, by in enumerate((0, 1, -1)):
        parts = (field[by, 0], field[by, 1], field[by, 2])
        parts += (field[by + 1, 0] if by < 2 else None, field[by - 1, 0])
        for i, part in enumerate(parts):
            at = (5 * g + i) * owned
            cand[at : at + owned, :] = part
    lane = iota((1, LANES), 1)
    at = iota((n, 1), 0)
    spread = jnp.zeros((n, LANES), F32)
    totals = jnp.zeros((1, LANES), F32)
    places = rows_ref[...].astype(jnp.int32)
    for p in range(count):
        row = gathered_ref[p, 3 * owned : 3 * owned + 1, :]
        if partial and p > 0:
            row = row + gathered_ref[p - 1, 3 * owned + 1 : 3 * owned + 2, :]
        if partial and p < count - 1:
            row = row + gathered_ref[p + 1, 3 * owned + 2 : 3 * owned + 3, :]
        totals = totals + row
        spread = spread + jnp.where(places[p : p + 1, :] == at, row, 0.0)
    right = jnp.sum(jnp.where(lane < total, spread, 0.0), axis=1, keepdims=True)
    coarse = jnp.sum(inverse_ref[...] * right, axis=0, keepdims=True)
    wide = iota((1, n), 1)
    right_row = jnp.sum(jnp.where(at == wide, right, 0.0), axis=0, keepdims=True)
    energy = jnp.sum(coarse * right_row, keepdims=True)
    totals = totals + jnp.where(lane == total + 2 * sweep, energy, 0.0)
    for ref in before:
        totals = totals + ref[...]
    sums_ref[...] = totals
    acc[...] = jnp.zeros_like(acc)
    acc[:owned, :] = field[0, 0]
    copy.wait()
    for g in range(3):
        gathered_rows(slots, corners, per, owned, g, facts, cand, u_ref)
    wide = wide.astype(F32)
    local = jnp.sum(field[0, 0] * field[0, 0], keepdims=True)
    for g in range(3):
        pack = packs[g]
        rows = (pack.shape[0] - 16) // slots
        tail = slots * rows
        for s in range(slots):
            panel = pack[s * rows : (s + 1) * rows, :].astype(BF16)
            u = u_ref[g * slots + s : g * slots + s + 1, :]
            t = row_times(u, panel, 1)
            weights = pack[tail + 8 + s : tail + 9 + s, :]
            if g == 0:
                local = local + jnp.sum(t * t, keepdims=True)
                local = local + jnp.sum(weights * u * u, keepdims=True)
            for i in range(corners // 8):
                first = s * corners + 8 * i
                place = places_ref[g * total + first : g * total + first + 8, :1]
                back = jnp.sum(jnp.where(place == wide, coarse, 0.0), axis=1, keepdims=True)
                j = first // 8
                part = pack[tail : tail + 8, j * LANES : (j + 1) * LANES]
                t = t + jnp.sum(back * part, axis=0, keepdims=True)
            w = row_times(t, panel, 0) + weights * u
            for b in range(per):
                k, sign = fact_of(facts, slots, corners, per, g, s, b, owned)
                acc[pl.ds(g * 5 * owned + k, 1), :] += w[:, b * LANES : (b + 1) * LANES] * sign
    mine[...] = acc[:owned, :] + acc[9 * owned : 10 * owned, :] + acc[13 * owned : 14 * owned, :]
    for ref in late:
        ref[...] = jnp.where(lane == total + 2 * sweep, local, 0.0)
    east[...] = acc[owned : 2 * owned, :]
    west[...] = acc[2 * owned : 3 * owned, :]


def final_kernel(first, x_ref, near_ref, far_ref, rhs_ref, v0, v1, v2, w0, w1, mine, m_ref, r_ref):
    run, runs_here = near_ref.shape[0], far_ref.shape[0]
    owned = mine.shape[0]
    x = x_ref[0]
    at, row = x % run, x // run
    low, high_end = slice(owned, 2 * owned), slice(2 * owned, 3 * owned)
    from_west = jnp.where(
        at > 0,
        near_ref[jnp.maximum(at - 1, 0), low, :],
        far_ref[jnp.maximum(row - 1, 0), low, :] * jnp.where(row > 0, 1.0, 0.0),
    )
    from_east = jnp.where(
        at < run - 1,
        near_ref[jnp.minimum(at + 1, run - 1), high_end, :],
        far_ref[jnp.minimum(row + 1, runs_here - 1), high_end, :]
        * jnp.where(row < runs_here - 1, 1.0, 0.0),
    )
    sums = jnp.sum(far_ref[:, 0, :], axis=0, keepdims=True)
    lane = iota((1, LANES), 1)

    def moment(i):
        return jnp.sum(jnp.where(lane == first + i, sums, 0.0), axis=1, keepdims=True)

    h00, r0, h11, h01, h22, h12 = (moment(i) for i in range(6))
    h02, r1, r2 = h11, STEP * h00, STEP * h01
    l10, l20 = h01 / h00, h02 / h00
    d1 = h11 - l10 * h01
    e12 = h12 - l10 * h02
    l21 = e12 / d1
    d2 = h22 - l20 * h02 - l21 * e12
    y1 = r1 - l10 * r0
    y2 = r2 - l20 * r0 - l21 * y1
    c2 = y2 / d2
    c1 = y1 / d1 - l21 * c2
    c0 = r0 / h00 - l10 * c1 - l20 * c2
    w2 = mine[...] + from_west + from_east
    m_ref[...] = c0 * v0[...] + c1 * v1[...] + c2 * v2[...]
    r_ref[...] = rhs_ref[...] - (c0 * w0[...] + c1 * w1[...] + c2 * w2)


def call(kernel, name, outs, scratch, scalars, arrays, space=pltpu.VMEM):
    vmem = pl.BlockSpec(memory_space=pltpu.VMEM)
    smem = pl.BlockSpec(memory_space=pltpu.SMEM)
    outs = [x if isinstance(x, jax.ShapeDtypeStruct) else jax.ShapeDtypeStruct(x, F32) for x in outs]
    return pl.pallas_call(
        kernel,
        out_shape=outs,
        in_specs=[smem] * len(scalars) + [pl.BlockSpec(memory_space=space)] * len(arrays),
        out_specs=[vmem] * len(outs),
        scratch_shapes=[pltpu.VMEM(x, F32) if isinstance(x, tuple) else x for x in scratch],
        compiler_params=pltpu.CompilerParams(vmem_limit_bytes=40 << 20),
        name=name,
    )(*scalars, *arrays)


def moved(x, axis, by):
    count = lax.axis_size(axis)
    return lax.ppermute(x, axis, [(i, i + by) for i in range(count) if 0 <= i + by < count])


def strided(count, by):
    return [list(range(i, count, by)) for i in range(by)]


def runs(count, size):
    return [list(range(i, i + size)) for i in range(0, count, size)]


def shards(
    panel, corner_panel, interface_diag, coarse_diag, scaling, dual_rhs, block_map, corner_map, counts
):
    slots, rows, width = panel.shape[2:]
    corners = corner_panel.shape[3]
    owned, block_size = scaling.shape[2:]
    n = coarse_diag.shape[1]
    total = slots * corners
    peers = lax.axis_size("gy")
    y = lax.axis_index("gy")
    per = block_map.shape[3]
    tile = (owned, block_size)
    facts_shape = jax.ShapeDtypeStruct((8, LANES), jnp.int32)
    facts_scratch = [pltpu.SMEM((8, LANES), jnp.int32), pltpu.SemaphoreType.DMA]
    rhs, scale = dual_rhs[0, 0], scaling[0, 0]
    direction = scale * rhs
    pack, report, corner_rows, facts = call(
        setup_kernel,
        "setup",
        [
            (slots * rows + 16, width),
            (corners + 8, LANES),
            (LANES, LANES),
            facts_shape,
        ],
        [
            pltpu.VMEM((slots, rows, width), BF16),
            pltpu.VMEM((slots, corners, rows), BF16),
            (slots, width),
            pltpu.VMEM((slots, corners), jnp.int32),
            pltpu.VMEM((slots, per), jnp.int32),
            pltpu.SMEM((1, 1), jnp.int32),
            (8, LANES),
            pltpu.SemaphoreType.DMA((6,)),
        ],
        [],
        [
            panel[0, 0],
            corner_panel[0, 0],
            interface_diag[0, 0],
            corner_map[0, 0],
            block_map[0, 0],
            counts,
        ],
        space=pltpu.HBM,
    )
    last = rhs
    directions, images, sums = [], [], []
    packs, late = [pack], []
    for sweep in range(3):
        partial = sweep == 1
        halo = [moved(direction, "gx", -1), moved(direction, "gx", 1)]
        if not partial:
            halo += [moved(direction, "gy", -1), moved(direction, "gy", 1)]
        extra = late if sweep else [report]
        size = 4 * owned + (0 if sweep else report.shape[0])
        groups = 3 if partial else 1
        (pay,) = call(
            functools.partial(before_kernel, slots, corners, per, sweep, groups, len(halo)),
            "before",
            [(size, LANES)],
            [(5 * groups * owned, block_size), (8, width), *facts_scratch],
            [],
            [
                direction,
                last,
                corner_rows,
                facts3 if partial else facts,
                *packs[:groups],
                *halo,
                *extra,
            ],
        )
        gathered = lax.all_gather(pay, "gy")
        if not sweep:
            here = y.reshape(1).astype(jnp.int32)
            started, place_rows, places3, facts3 = call(
                functools.partial(coarse_kernel, slots, corners, 4 * owned),
                "coarse",
                [(n, n), (peers, LANES), (3 * total, LANES), facts_shape],
                [(peers * total, n), (peers * total, n)],
                [here],
                [gathered, coarse_diag],
            )
            started, leaving = lax.optimization_barrier((started, pack))
            packs = [pack, moved(leaving, "gy", -1), moved(leaving, "gy", 1)]
            (inverse,) = call(rest_kernel, "rest", [(n, n)], [], [], [started])
        outs = [tile] * 3 + [(1, LANES)] * (2 if partial else 1)
        if sweep == 2:
            outs = [tile, (3 * owned, LANES)]
        mine, *outs = call(
            functools.partial(after_kernel, slots, corners, per, sweep, partial),
            "after",
            outs,
            [(15 * owned, block_size), (8, width), (15 * owned, block_size), *facts_scratch],
            [here],
            [gathered, place_rows, places3, facts3, inverse, *packs, *([sums] if sweep else [])],
        )
        if sweep < 2:
            east, west, sums, *late = outs
            arrived = [moved(east, "gx", 1), moved(west, "gx", -1)]
        directions.append(direction)
        if sweep < 2:
            image = mine + arrived[0] + arrived[1]
            images.append(image)
            last, direction = image, STEP * scale * image
    across, run = lax.axis_size("gx"), 4
    near = lax.all_gather(outs[0], "gx", axis_index_groups=runs(across, run))
    ends = jnp.concatenate(
        [
            jnp.sum(near[:, :owned], axis=0),
            near[run - 1, owned : 2 * owned],
            near[0, 2 * owned :],
        ],
        axis=0,
    )
    far = lax.all_gather(ends, "gx", axis_index_groups=strided(across, run))
    place = lax.axis_index("gx").reshape(1).astype(jnp.int32)
    multipliers, residual = call(
        functools.partial(final_kernel, total),
        "final",
        [tile] * 2,
        [],
        [place],
        [near, far, rhs, *directions, *images, mine],
    )
    return multipliers[None, None], residual[None, None]


def solution(mesh):
    return jax.shard_map(
        shards,
        mesh=mesh,
        in_specs=(
            P("gx", "gy", None, None, None),
            P("gx", "gy", None, None, None),
            P("gx", "gy", None, None),
            P("gx", None),
            P("gx", "gy", None, None),
            P("gx", "gy", None, None),
            P("gx", "gy", None, None),
            P("gx", "gy", None, None),
            P("gx", "gy"),
        ),
        out_specs=(P("gx", "gy", None, None), P("gx", "gy", None, None)),
        check_vma=False,
    )
```

```python
import functools

import jax
import jax.numpy as jnp
from jax import lax
from jax.experimental import pallas as pl
from jax.experimental.pallas import tpu as pltpu
from jax.sharding import PartitionSpec as P

F32 = jnp.float32
BF16 = jnp.bfloat16
STEP = 0.00390625
LANES = 128
PIVOTS = 4


def iota(shape, dim):
    return lax.broadcasted_iota(jnp.int32, shape, dim)


def high(a, b):
    return jnp.dot(a, b, precision=lax.Precision.HIGHEST, preferred_element_type=F32)


def thirds(x):
    first = x.astype(BF16).astype(F32)
    rest = x - first
    second = rest.astype(BF16).astype(F32)
    return first, second, rest - second


def stacked(row):
    first, second, third = thirds(row)
    at = iota((16, 1), 0)
    rows = jnp.where(at == 0, first, jnp.where(at == 1, second, jnp.where(at == 2, third, 0.0)))
    return rows.astype(BF16)


def row_times(row, matrix, dim):
    out = lax.dot_general(
        stacked(row), matrix, (((1,), (dim,)), ((), ())), preferred_element_type=F32
    )
    return jnp.sum(out[:8], axis=0, keepdims=True)


def exact_times(x, hot):
    return sum(jnp.dot(piece.astype(BF16), hot, preferred_element_type=F32) for piece in thirds(x))


def inverse2(a, b, c):
    r = 1.0 / (a * c - b * b)
    return c * r, -b * r, a * r


def pivot_inverse(e):
    p = inverse2(e(0, 0), e(0, 1), e(1, 1))
    b = [[e(0, 2), e(0, 3)], [e(1, 2), e(1, 3)]]
    u = [
        [p[0] * b[0][j] + p[1] * b[1][j] for j in (0, 1)],
        [p[1] * b[0][j] + p[2] * b[1][j] for j in (0, 1)],
    ]
    s = inverse2(
        e(2, 2) - (b[0][0] * u[0][0] + b[1][0] * u[1][0]),
        e(2, 3) - (b[0][0] * u[0][1] + b[1][0] * u[1][1]),
        e(3, 3) - (b[0][1] * u[0][1] + b[1][1] * u[1][1]),
    )
    x = [[u[i][0] * s[0] + u[i][1] * s[1], u[i][0] * s[1] + u[i][1] * s[2]] for i in (0, 1)]
    p00 = p[0] + x[0][0] * u[0][0] + x[0][1] * u[0][1]
    p01 = p[1] + x[0][0] * u[1][0] + x[0][1] * u[1][1]
    p11 = p[2] + x[1][0] * u[1][0] + x[1][1] * u[1][1]
    return [
        [p00, p01, -x[0][0], -x[0][1]],
        [p01, p11, -x[1][0], -x[1][1]],
        [-x[0][0], -x[1][0], s[0], s[1]],
        [-x[0][1], -x[1][1], s[1], s[2]],
    ]


def small_inverse(a, n):
    lane = iota((1, n), 1)
    at8 = iota((8, 1), 0)
    for k in range(0, n, PIVOTS):
        rows = [a[k + i : k + i + 1, :] for i in range(PIVOTS)]
        cols = [jnp.broadcast_to(a[:, k + i : k + i + 1], (n, n)) for i in range(PIVOTS)]
        w = pivot_inverse(lambda i, j: cols[j][k + i : k + i + 1, :])
        inside = (lane >= k) & (lane < k + PIVOTS)
        units = [
            jnp.where(inside, jnp.where(lane == k + i, 1.0, 0.0), rows[i]) for i in range(PIVOTS)
        ]
        fresh = [sum(w[i][j] * units[j] for j in range(PIVOTS)) for i in range(PIVOTS)]
        base = jnp.where(inside, 0.0, a)
        for i in range(PIVOTS):
            base = base - cols[i] * fresh[i]
        v = k // 8 * 8
        block = base[v : v + 8]
        for i in range(PIVOTS):
            block = jnp.where(at8 == k + i - v, fresh[i], block)
        a = jnp.concatenate([x for x in (base[:v], block, base[v + 8 :]) if x.shape[0]], axis=0)
    return a


def setup_kernel(
    panel_hbm, corner_hbm, diag_hbm, place_hbm, map_hbm, count_hbm, pack_ref, report_ref, rows_ref, facts_ref, panel_ref, corner_ref, diag_ref,
    place_ref, map_ref, count_ref, facts, sems,
):
    slots, rows, width = panel_ref.shape
    corners = corner_ref.shape[1]
    per = map_ref.shape[1]
    total = slots * corners
    at = slots * rows
    moves = (
        (corner_hbm, corner_ref),
        (place_hbm, place_ref),
        (map_hbm, map_ref),
        (count_hbm, count_ref),
        (diag_hbm, diag_ref),
        (panel_hbm, panel_ref),
    )
    copies = [pltpu.make_async_copy(a, b, sems.at[i]) for i, (a, b) in enumerate(moves)]
    for copy in copies:
        copy.start()
    pack_ref[at:, :] = jnp.zeros((16, width), F32)
    rows_ref[...] = jnp.zeros_like(rows_ref)
    facts[...] = jnp.zeros_like(facts)
    for copy in copies:
        copy.wait()
    pack_ref[at + 8 : at + 8 + slots, :] = diag_ref[...]
    lane = iota((1, LANES), 1)
    for s in range(slots):
        pack_ref[s * rows : (s + 1) * rows, :] = panel_ref[s].astype(F32)
        rows_ref[s * corners : (s + 1) * corners, :] = corner_ref[s].astype(F32)
        facts[s : s + 1, :corners] = place_ref[s : s + 1, :].astype(F32)
        facts[slots + s : slots + s + 1, :per] = map_ref[s : s + 1, :].astype(F32)
    for i in range(total // 8):
        pack_ref[at : at + 8, i * LANES : (i + 1) * LANES] = rows_ref[8 * i : 8 * i + 8, :]
    narrow = rows_ref[...].astype(BF16)
    square = lax.dot_general(
        narrow, narrow, (((1,), (1,)), ((), ())), preferred_element_type=F32
    )
    part = jnp.zeros((corners, LANES), F32)
    count = count_ref[0, 0]
    fact = jnp.where(lane == total + slots * per, count.astype(F32), 0.0)
    for s in range(slots):
        live = jnp.where(s < count, 1.0, 0.0)
        first = s * corners
        mine = (lane >= first) & (lane < first + corners)
        part = jnp.where(mine, square[first : first + corners, :] * live, part)
        row = facts[s : s + 1, :]
        column = jnp.sum(
            jnp.where(iota((corners, 1), 0) == lane, row, 0.0), axis=1, keepdims=True
        )
        part = jnp.where(lane == total + s, column, part)
        fact = fact + (pltpu.roll(row, first, 1) if s else row)
        fact = fact + pltpu.roll(facts[slots + s : slots + s + 1, :], total + s * per, 1)
    report_ref[...] = part
    facts_ref[...] = jnp.broadcast_to(fact.astype(jnp.int32), (8, LANES))


def flipped(a, b):
    return lax.dot_general(
        a, b, (((1,), (1,)), ((), ())), precision=lax.Precision.HIGHEST, preferred_element_type=F32
    )


def split_inverse(m, n):
    h = n // 2
    a, b, bt, c = m[:h, :h], m[:h, h:], m[h:, :h], m[h:, h:]
    ai = small_inverse(a, h)
    u = high(ai, b)
    si = small_inverse(c - high(bt, u), h)
    x, xt = high(u, si), flipped(si, u)
    top = jnp.concatenate([ai + flipped(x, u), -x], axis=1)
    return jnp.concatenate([top, jnp.concatenate([-xt, si], axis=1)], axis=0)


def coarse_kernel(
    slots, corners, start, y_ref, gathered_ref, diag_ref, out_ref, rows_ref, places_ref, facts_ref,
    hot_ref, spread_ref,
):
    count = gathered_ref.shape[0]
    total = slots * corners
    told = start * 3 // 4 + 1
    n = diag_ref.shape[1]
    lane = iota((1, n), 1).astype(F32)
    for y in range(count):
        part = gathered_ref[y, start : start + corners, :]
        rows_ref[y : y + 1, :] = gathered_ref[y, told : told + 1, :]
        for s in range(slots):
            block = part[:, s * corners : (s + 1) * corners]
            place = part[:, total + s : total + s + 1]
            hot = jnp.where(place == lane, 1.0, 0.0)
            at = (y * slots + s) * corners
            hot_ref[at : at + corners, :] = hot
            spread_ref[at : at + corners, :] = exact_times(block, hot.astype(BF16))
    facts_ref[...] = jnp.zeros_like(facts_ref)
    for g, by in enumerate((0, 1, -1)):
        there = y_ref[0] + by
        y = jnp.clip(there, 0, count - 1)
        fact = gathered_ref[y, told : told + 1, :].astype(jnp.int32)
        facts_ref[g : g + 1, :] = jnp.where((there >= 0) & (there < count), fact, 0)
        part = gathered_ref[y, start : start + corners, :]
        for s in range(slots):
            at = g * total + s * corners
            places_ref[at : at + corners, :] = jnp.broadcast_to(
                part[:, total + s : total + s + 1], (corners, LANES)
            )
    hots = hot_ref[...].astype(BF16)
    system = jnp.where(iota((n, 1), 0) == iota((1, n), 1), diag_ref[...], 0.0)
    for piece in thirds(spread_ref[...]):
        system = system + lax.dot_general(
            hots, piece.astype(BF16), (((0,), (0,)), ((), ())), preferred_element_type=F32
        )
    out_ref[...] = system
    eliminated(out_ref, 0, 1)


def rest_kernel(system_ref, out_ref):
    out_ref[...] = system_ref[...]
    eliminated(out_ref, 1, out_ref.shape[0] // LANES)


def eliminated(out_ref, first, last):
    n = out_ref.shape[0]
    b = LANES

    def eliminate(k, carry):
        ro = pl.multiple_of(k * b, b)
        pivots = split_inverse(out_ref[pl.ds(ro, b), pl.ds(ro, b)], b)
        col = out_ref[:, pl.ds(ro, b)]
        out_ref[:, pl.ds(ro, b)] = jnp.zeros((n, b), F32)
        out_ref[pl.ds(ro, b), pl.ds(ro, b)] = jnp.where(iota((b, b), 0) == iota((b, b), 1), 1.0, 0.0)
        fresh = high(pivots, out_ref[pl.ds(ro, b), :])
        out_ref[pl.ds(ro, b), :] = jnp.zeros((b, n), F32)
        at = iota((n, 1), 0)
        others = jnp.where((at >= ro) & (at < ro + b), 0.0, col)
        out_ref[...] = out_ref[...] - high(others, fresh)
        out_ref[pl.ds(ro, b), :] = fresh
        return carry

    lax.fori_loop(first, last, eliminate, 0)


def fact_of(facts, slots, corners, per, g, s, b, owned):
    k = facts[g, slots * corners + s * per + b]
    live = jnp.where(s < facts[g, slots * corners + slots * per], 1.0, 0.0)
    return k, jnp.where(k < owned, live, -live)


def gathered_rows(slots, corners, per, owned, g, facts, cand, u_ref):
    for s in range(slots):
        for b in range(per):
            k, sign = fact_of(facts, slots, corners, per, g, s, b, owned)
            row = cand[pl.ds(g * 5 * owned + k, 1), :] * sign
            u_ref[g * slots + s : g * slots + s + 1, b * LANES : (b + 1) * LANES] = row


def before_kernel(slots, corners, per, sweep, groups, parts, v_ref, last_ref, corner_ref, facts_ref, *rest):
    rest, (pay_ref, cand, u_ref, facts, sem) = rest[:-5], rest[-5:]
    packs, halo, extra = rest[:groups], rest[groups : groups + parts], rest[groups + parts :]
    copy = pltpu.make_async_copy(facts_ref, facts, sem)
    copy.start()
    owned = v_ref.shape[0]
    total = slots * corners
    v = v_ref[...]
    if groups > 1:
        cand[...] = jnp.zeros_like(cand)
        cand[9 * owned : 10 * owned, :] = v
        cand[13 * owned : 14 * owned, :] = v
    for i, ref in enumerate((v_ref, *halo)):
        cand[i * owned : (i + 1) * owned, :] = ref[...]
        if i < 3:
            pay_ref[i * owned : (i + 1) * owned, :] = ref[...]
    at = iota((owned, 1), 0)
    lane = iota((1, LANES), 1)
    energy = jnp.sum(v * v, keepdims=True)
    pays = []
    copy.wait()
    for g in range(groups):
        pack = packs[g]
        rows = (pack.shape[0] - 16) // slots
        pay = jnp.zeros((1, LANES), F32)
        gathered_rows(slots, corners, per, owned, g, facts, cand, u_ref)
        for s in range(slots):
            live = jnp.where(s < facts[g, total + slots * per], 1.0, 0.0)
            u = u_ref[g * slots + s : g * slots + s + 1, :]
            t = row_times(u, pack[s * rows : (s + 1) * rows, :].astype(BF16), 1)
            energy = energy + jnp.sum(t * t, keepdims=True)
            weights = pack[slots * rows + 8 + s : slots * rows + 9 + s, :]
            energy = energy + jnp.sum(weights * u * u, keepdims=True)
            first = s * corners
            if g:
                j = slots * rows
                narrow = [
                    pack[j : j + 8, i * LANES : (i + 1) * LANES] for i in range(total // 8)
                ]
                narrow = jnp.concatenate(narrow + [jnp.zeros((LANES - total, LANES), F32)], axis=0)
            else:
                narrow = corner_ref[...]
            c = row_times(t, narrow.astype(BF16), 1) * live
            pay = jnp.where((lane >= first) & (lane < first + corners), c, pay)
        pays.append(pay)
    cross = jnp.sum(v * last_ref[...], keepdims=True)
    pay = pays[0]
    if groups == 1:
        pay = jnp.where(lane == total + 2 * sweep, energy, pay)
    pay = jnp.where(lane == total + 2 * sweep + 1, cross, pay)
    for ref in extra:
        if ref.shape[0] == 1:
            pay = pay + ref[...]
        else:
            pay_ref[4 * owned :, :] = ref[...]
    block = jnp.where(at == 0, pay, 0.0)
    if not sweep:
        block = jnp.where(at == 1, facts_ref[:1, :].astype(F32), block)
    for g in range(1, groups):
        block = jnp.where(at == g, pays[g], block)
    pay_ref[3 * owned : 4 * owned, :] = block


def after_kernel(
    slots, corners, per, sweep, partial, y_ref, gathered_ref, rows_ref, places_ref, facts_ref, inverse_ref,
    *rest,
):
    packs, rest = rest[:3], rest[3:]
    before, rest = rest[: 1 if sweep else 0], rest[1 if sweep else 0 :]
    late, (cand, u_ref, acc, facts, sem) = rest[4:-5], rest[-5:]
    mine, east, west, sums_ref = rest[:4]
    copy = pltpu.make_async_copy(facts_ref, facts, sem)
    copy.start()
    owned = mine.shape[0]
    total = slots * corners
    n = inverse_ref.shape[0]
    count = gathered_ref.shape[0]
    middle = y_ref[0]
    field = {}
    for by in (0, 1, -1, 2, -2):
        y = middle + by
        inside = jnp.where((y >= 0) & (y < count), 1.0, 0.0)
        p = jnp.clip(y, 0, count - 1)
        for i in range(3 if abs(by) < 2 else 1):
            field[by, i] = gathered_ref[p, i * owned : (i + 1) * owned, :] * inside
    for g, by in enumerate((0, 1, -1)):
        parts = (field[by, 0], field[by, 1], field[by, 2])
        parts += (field[by + 1, 0] if by < 2 else None, field[by - 1, 0])
        for i, part in enumerate(parts):
            at = (5 * g + i) * owned
            cand[at : at + owned, :] = part
    lane = iota((1, LANES), 1)
    at = iota((n, 1), 0)
    spread = jnp.zeros((n, LANES), F32)
    totals = jnp.zeros((1, LANES), F32)
    places = rows_ref[...].astype(jnp.int32)
    for p in range(count):
        row = gathered_ref[p, 3 * owned : 3 * owned + 1, :]
        if partial and p > 0:
            row = row + gathered_ref[p - 1, 3 * owned + 1 : 3 * owned + 2, :]
        if partial and p < count - 1:
            row = row + gathered_ref[p + 1, 3 * owned + 2 : 3 * owned + 3, :]
        totals = totals + row
        spread = spread + jnp.where(places[p : p + 1, :] == at, row, 0.0)
    right = jnp.sum(jnp.where(lane < total, spread, 0.0), axis=1, keepdims=True)
    coarse = jnp.sum(inverse_ref[...] * right, axis=0, keepdims=True)
    wide = iota((1, n), 1)
    right_row = jnp.sum(jnp.where(at == wide, right, 0.0), axis=0, keepdims=True)
    energy = jnp.sum(coarse * right_row, keepdims=True)
    totals = totals + jnp.where(lane == total + 2 * sweep, energy, 0.0)
    for ref in before:
        totals = totals + ref[...]
    sums_ref[...] = totals
    acc[...] = jnp.zeros_like(acc)
    acc[:owned, :] = field[0, 0]
    copy.wait()
    for g in range(3):
        gathered_rows(slots, corners, per, owned, g, facts, cand, u_ref)
    wide = wide.astype(F32)
    local = jnp.sum(field[0, 0] * field[0, 0], keepdims=True)
    for g in range(3):
        pack = packs[g]
        rows = (pack.shape[0] - 16) // slots
        tail = slots * rows
        for s in range(slots):
            panel = pack[s * rows : (s + 1) * rows, :].astype(BF16)
            u = u_ref[g * slots + s : g * slots + s + 1, :]
            t = row_times(u, panel, 1)
            weights = pack[tail + 8 + s : tail + 9 + s, :]
            if g == 0:
                local = local + jnp.sum(t * t, keepdims=True)
                local = local + jnp.sum(weights * u * u, keepdims=True)
            for i in range(corners // 8):
                first = s * corners + 8 * i
                place = places_ref[g * total + first : g * total + first + 8, :1]
                back = jnp.sum(jnp.where(place == wide, coarse, 0.0), axis=1, keepdims=True)
                j = first // 8
                part = pack[tail : tail + 8, j * LANES : (j + 1) * LANES]
                t = t + jnp.sum(back * part, axis=0, keepdims=True)
            w = row_times(t, panel, 0) + weights * u
            for b in range(per):
                k, sign = fact_of(facts, slots, corners, per, g, s, b, owned)
                acc[pl.ds(g * 5 * owned + k, 1), :] += w[:, b * LANES : (b + 1) * LANES] * sign
    mine[...] = acc[:owned, :] + acc[9 * owned : 10 * owned, :] + acc[13 * owned : 14 * owned, :]
    for ref in late:
        ref[...] = jnp.where(lane == total + 2 * sweep, local, 0.0)
    east[...] = acc[owned : 2 * owned, :]
    west[...] = acc[2 * owned : 3 * owned, :]


def final_kernel(first, gathered_ref, rhs_ref, v0, v1, v2, w0, w1, mine, east, west, x_ref, r_ref):
    sums = jnp.sum(gathered_ref[...], axis=0, keepdims=True)
    lane = iota((1, LANES), 1)

    def moment(i):
        return jnp.sum(jnp.where(lane == first + i, sums, 0.0), axis=1, keepdims=True)

    h00, r0, h11, h01, h22, h12 = (moment(i) for i in range(6))
    h02, r1, r2 = h11, STEP * h00, STEP * h01
    l10, l20 = h01 / h00, h02 / h00
    d1 = h11 - l10 * h01
    e12 = h12 - l10 * h02
    l21 = e12 / d1
    d2 = h22 - l20 * h02 - l21 * e12
    y1 = r1 - l10 * r0
    y2 = r2 - l20 * r0 - l21 * y1
    c2 = y2 / d2
    c1 = y1 / d1 - l21 * c2
    c0 = r0 / h00 - l10 * c1 - l20 * c2
    w2 = mine[...] + east[...] + west[...]
    x_ref[...] = c0 * v0[...] + c1 * v1[...] + c2 * v2[...]
    r_ref[...] = rhs_ref[...] - (c0 * w0[...] + c1 * w1[...] + c2 * w2)


def call(kernel, name, outs, scratch, scalars, arrays, space=pltpu.VMEM):
    vmem = pl.BlockSpec(memory_space=pltpu.VMEM)
    smem = pl.BlockSpec(memory_space=pltpu.SMEM)
    outs = [x if isinstance(x, jax.ShapeDtypeStruct) else jax.ShapeDtypeStruct(x, F32) for x in outs]
    return pl.pallas_call(
        kernel,
        out_shape=outs,
        in_specs=[smem] * len(scalars) + [pl.BlockSpec(memory_space=space)] * len(arrays),
        out_specs=[vmem] * len(outs),
        scratch_shapes=[pltpu.VMEM(x, F32) if isinstance(x, tuple) else x for x in scratch],
        compiler_params=pltpu.CompilerParams(vmem_limit_bytes=40 << 20),
        name=name,
    )(*scalars, *arrays)


def moved(x, axis, by):
    count = lax.axis_size(axis)
    return lax.ppermute(x, axis, [(i, i + by) for i in range(count) if 0 <= i + by < count])


def strided(count, by):
    return [list(range(i, count, by)) for i in range(by)]


def runs(count, size):
    return [list(range(i, i + size)) for i in range(0, count, size)]


def shards(
    panel, corner_panel, interface_diag, coarse_diag, scaling, dual_rhs, block_map, corner_map, counts
):
    slots, rows, width = panel.shape[2:]
    corners = corner_panel.shape[3]
    owned, block_size = scaling.shape[2:]
    n = coarse_diag.shape[1]
    total = slots * corners
    peers = lax.axis_size("gy")
    y = lax.axis_index("gy")
    per = block_map.shape[3]
    tile = (owned, block_size)
    facts_shape = jax.ShapeDtypeStruct((8, LANES), jnp.int32)
    facts_scratch = [pltpu.SMEM((8, LANES), jnp.int32), pltpu.SemaphoreType.DMA]
    rhs, scale = dual_rhs[0, 0], scaling[0, 0]
    direction = scale * rhs
    pack, report, corner_rows, facts = call(
        setup_kernel,
        "setup",
        [
            (slots * rows + 16, width),
            (corners, LANES),
            (LANES, LANES),
            facts_shape,
        ],
        [
            pltpu.VMEM((slots, rows, width), BF16),
            pltpu.VMEM((slots, corners, rows), BF16),
            (slots, width),
            pltpu.VMEM((slots, corners), jnp.int32),
            pltpu.VMEM((slots, per), jnp.int32),
            pltpu.SMEM((1, 1), jnp.int32),
            (8, LANES),
            pltpu.SemaphoreType.DMA((6,)),
        ],
        [],
        [
            panel[0, 0],
            corner_panel[0, 0],
            interface_diag[0, 0],
            corner_map[0, 0],
            block_map[0, 0],
            counts,
        ],
        space=pltpu.HBM,
    )
    last = rhs
    directions, images, sums = [], [], []
    packs, late = [pack], []
    for sweep in range(3):
        partial = sweep == 1
        halo = [moved(direction, "gx", -1), moved(direction, "gx", 1)]
        if not partial:
            halo += [moved(direction, "gy", -1), moved(direction, "gy", 1)]
        extra = late if sweep else [report]
        size = 4 * owned + (0 if sweep else report.shape[0])
        groups = 3 if partial else 1
        (pay,) = call(
            functools.partial(before_kernel, slots, corners, per, sweep, groups, len(halo)),
            "before",
            [(size, LANES)],
            [(5 * groups * owned, block_size), (8, width), *facts_scratch],
            [],
            [
                direction,
                last,
                corner_rows,
                facts3 if partial else facts,
                *packs[:groups],
                *halo,
                *extra,
            ],
        )
        gathered = lax.all_gather(pay, "gy")
        if not sweep:
            here = y.reshape(1).astype(jnp.int32)
            started, place_rows, places3, facts3 = call(
                functools.partial(coarse_kernel, slots, corners, 4 * owned),
                "coarse",
                [(n, n), (peers, LANES), (3 * total, LANES), facts_shape],
                [(peers * total, n), (peers * total, n)],
                [here],
                [gathered, coarse_diag],
            )
            started, leaving = lax.optimization_barrier((started, pack))
            packs = [pack, moved(leaving, "gy", -1), moved(leaving, "gy", 1)]
            (inverse,) = call(rest_kernel, "rest", [(n, n)], [], [], [started])
        mine, east, west, sums, *late = call(
            functools.partial(after_kernel, slots, corners, per, sweep, partial),
            "after",
            [tile] * 3 + [(1, LANES)] * (2 if partial else 1),
            [(15 * owned, block_size), (8, width), (15 * owned, block_size), *facts_scratch],
            [here],
            [gathered, place_rows, places3, facts3, inverse, *packs, *([sums] if sweep else [])],
        )
        arrived = [moved(east, "gx", 1), moved(west, "gx", -1)]
        directions.append(direction)
        if sweep < 2:
            image = mine + arrived[0] + arrived[1]
            images.append(image)
            last, direction = image, STEP * scale * image
    across = lax.axis_size("gx")
    sums = lax.all_gather(sums, "gx", axis=0, tiled=True, axis_index_groups=runs(across, 4))
    sums = jnp.sum(sums, axis=0, keepdims=True)
    sums = lax.all_gather(sums, "gx", axis=0, tiled=True, axis_index_groups=strided(across, 4))
    multipliers, residual = call(
        functools.partial(final_kernel, total),
        "final",
        [tile] * 2,
        [],
        [],
        [sums, rhs, *directions, *images, mine, *arrived],
    )
    return multipliers[None, None], residual[None, None]


def solution(mesh):
    return jax.shard_map(
        shards,
        mesh=mesh,
        in_specs=(
            P("gx", "gy", None, None, None),
            P("gx", "gy", None, None, None),
            P("gx", "gy", None, None),
            P("gx", None),
            P("gx", "gy", None, None),
            P("gx", "gy", None, None),
            P("gx", "gy", None, None),
            P("gx", "gy", None, None),
            P("gx", "gy"),
        ),
        out_specs=(P("gx", "gy", None, None), P("gx", "gy", None, None)),
        check_vma=False,
    )
```

```python
import functools

import jax
import jax.numpy as jnp
from jax import lax
from jax.experimental import pallas as pl
from jax.experimental.pallas import tpu as pltpu
from jax.sharding import PartitionSpec as P

F32 = jnp.float32
BF16 = jnp.bfloat16
STEP = 0.00390625
LANES = 128
PIVOTS = 4


def iota(shape, dim):
    return lax.broadcasted_iota(jnp.int32, shape, dim)


def high(a, b):
    return jnp.dot(a, b, precision=lax.Precision.HIGHEST, preferred_element_type=F32)


def thirds(x):
    first = x.astype(BF16).astype(F32)
    rest = x - first
    second = rest.astype(BF16).astype(F32)
    return first, second, rest - second


def stacked(row):
    first, second, third = thirds(row)
    at = iota((16, 1), 0)
    rows = jnp.where(at == 0, first, jnp.where(at == 1, second, jnp.where(at == 2, third, 0.0)))
    return rows.astype(BF16)


def row_times(row, matrix, dim):
    out = lax.dot_general(
        stacked(row), matrix, (((1,), (dim,)), ((), ())), preferred_element_type=F32
    )
    return jnp.sum(out[:8], axis=0, keepdims=True)


def exact_times(x, hot):
    return sum(jnp.dot(piece.astype(BF16), hot, preferred_element_type=F32) for piece in thirds(x))


def inverse2(a, b, c):
    r = 1.0 / (a * c - b * b)
    return c * r, -b * r, a * r


def pivot_inverse(e):
    p = inverse2(e(0, 0), e(0, 1), e(1, 1))
    b = [[e(0, 2), e(0, 3)], [e(1, 2), e(1, 3)]]
    u = [
        [p[0] * b[0][j] + p[1] * b[1][j] for j in (0, 1)],
        [p[1] * b[0][j] + p[2] * b[1][j] for j in (0, 1)],
    ]
    s = inverse2(
        e(2, 2) - (b[0][0] * u[0][0] + b[1][0] * u[1][0]),
        e(2, 3) - (b[0][0] * u[0][1] + b[1][0] * u[1][1]),
        e(3, 3) - (b[0][1] * u[0][1] + b[1][1] * u[1][1]),
    )
    x = [[u[i][0] * s[0] + u[i][1] * s[1], u[i][0] * s[1] + u[i][1] * s[2]] for i in (0, 1)]
    p00 = p[0] + x[0][0] * u[0][0] + x[0][1] * u[0][1]
    p01 = p[1] + x[0][0] * u[1][0] + x[0][1] * u[1][1]
    p11 = p[2] + x[1][0] * u[1][0] + x[1][1] * u[1][1]
    return [
        [p00, p01, -x[0][0], -x[0][1]],
        [p01, p11, -x[1][0], -x[1][1]],
        [-x[0][0], -x[1][0], s[0], s[1]],
        [-x[0][1], -x[1][1], s[1], s[2]],
    ]


def small_inverse(a, n):
    lane = iota((1, n), 1)
    at8 = iota((8, 1), 0)
    for k in range(0, n, PIVOTS):
        rows = [a[k + i : k + i + 1, :] for i in range(PIVOTS)]
        cols = [jnp.broadcast_to(a[:, k + i : k + i + 1], (n, n)) for i in range(PIVOTS)]
        w = pivot_inverse(lambda i, j: cols[j][k + i : k + i + 1, :])
        inside = (lane >= k) & (lane < k + PIVOTS)
        units = [
            jnp.where(inside, jnp.where(lane == k + i, 1.0, 0.0), rows[i]) for i in range(PIVOTS)
        ]
        fresh = [sum(w[i][j] * units[j] for j in range(PIVOTS)) for i in range(PIVOTS)]
        base = jnp.where(inside, 0.0, a)
        for i in range(PIVOTS):
            base = base - cols[i] * fresh[i]
        v = k // 8 * 8
        block = base[v : v + 8]
        for i in range(PIVOTS):
            block = jnp.where(at8 == k + i - v, fresh[i], block)
        a = jnp.concatenate([x for x in (base[:v], block, base[v + 8 :]) if x.shape[0]], axis=0)
    return a


def setup_kernel(
    panel_hbm, corner_hbm, diag_hbm, place_hbm, map_hbm, count_hbm, pack_ref, report_ref, rows_ref, facts_ref, panel_ref, corner_ref, diag_ref,
    place_ref, map_ref, count_ref, facts, sems,
):
    slots, rows, width = panel_ref.shape
    corners = corner_ref.shape[1]
    per = map_ref.shape[1]
    total = slots * corners
    at = slots * rows
    moves = (
        (corner_hbm, corner_ref),
        (place_hbm, place_ref),
        (map_hbm, map_ref),
        (count_hbm, count_ref),
        (diag_hbm, diag_ref),
        (panel_hbm, panel_ref),
    )
    copies = [pltpu.make_async_copy(a, b, sems.at[i]) for i, (a, b) in enumerate(moves)]
    for copy in copies:
        copy.start()
    pack_ref[at:, :] = jnp.zeros((16, width), F32)
    rows_ref[...] = jnp.zeros_like(rows_ref)
    facts[...] = jnp.zeros_like(facts)
    for copy in copies:
        copy.wait()
    pack_ref[at + 8 : at + 8 + slots, :] = diag_ref[...]
    lane = iota((1, LANES), 1)
    for s in range(slots):
        pack_ref[s * rows : (s + 1) * rows, :] = panel_ref[s].astype(F32)
        rows_ref[s * corners : (s + 1) * corners, :] = corner_ref[s].astype(F32)
        facts[s : s + 1, :corners] = place_ref[s : s + 1, :].astype(F32)
        facts[slots + s : slots + s + 1, :per] = map_ref[s : s + 1, :].astype(F32)
    for i in range(total // 8):
        pack_ref[at : at + 8, i * LANES : (i + 1) * LANES] = rows_ref[8 * i : 8 * i + 8, :]
    narrow = rows_ref[...].astype(BF16)
    square = lax.dot_general(
        narrow, narrow, (((1,), (1,)), ((), ())), preferred_element_type=F32
    )
    part = jnp.zeros((corners, LANES), F32)
    count = count_ref[0, 0]
    fact = jnp.where(lane == total + slots * per, count.astype(F32), 0.0)
    for s in range(slots):
        live = jnp.where(s < count, 1.0, 0.0)
        first = s * corners
        mine = (lane >= first) & (lane < first + corners)
        part = jnp.where(mine, square[first : first + corners, :] * live, part)
        row = facts[s : s + 1, :]
        column = jnp.sum(
            jnp.where(iota((corners, 1), 0) == lane, row, 0.0), axis=1, keepdims=True
        )
        part = jnp.where(lane == total + s, column, part)
        fact = fact + (pltpu.roll(row, first, 1) if s else row)
        fact = fact + pltpu.roll(facts[slots + s : slots + s + 1, :], total + s * per, 1)
    report_ref[:corners, :] = part
    report_ref[corners:, :] = jnp.broadcast_to(fact, (8, LANES))
    facts_ref[...] = jnp.broadcast_to(fact.astype(jnp.int32), (8, LANES))


def flipped(a, b):
    return lax.dot_general(
        a, b, (((1,), (1,)), ((), ())), precision=lax.Precision.HIGHEST, preferred_element_type=F32
    )


def split_inverse(m, n):
    h = n // 2
    a, b, bt, c = m[:h, :h], m[:h, h:], m[h:, :h], m[h:, h:]
    ai = small_inverse(a, h)
    u = high(ai, b)
    si = small_inverse(c - high(bt, u), h)
    x, xt = high(u, si), flipped(si, u)
    top = jnp.concatenate([ai + flipped(x, u), -x], axis=1)
    return jnp.concatenate([top, jnp.concatenate([-xt, si], axis=1)], axis=0)


def coarse_kernel(
    slots, corners, start, y_ref, gathered_ref, diag_ref, out_ref, rows_ref, places_ref, facts_ref,
    hot_ref, spread_ref,
):
    count = gathered_ref.shape[0]
    total = slots * corners
    n = diag_ref.shape[1]
    lane = iota((1, n), 1).astype(F32)
    for y in range(count):
        part = gathered_ref[y, start : start + corners, :]
        rows_ref[y : y + 1, :] = gathered_ref[y, start + corners : start + corners + 1, :]
        for s in range(slots):
            block = part[:, s * corners : (s + 1) * corners]
            place = part[:, total + s : total + s + 1]
            hot = jnp.where(place == lane, 1.0, 0.0)
            at = (y * slots + s) * corners
            hot_ref[at : at + corners, :] = hot
            spread_ref[at : at + corners, :] = exact_times(block, hot.astype(BF16))
    facts_ref[...] = jnp.zeros_like(facts_ref)
    for g, by in enumerate((0, 1, -1)):
        there = y_ref[0] + by
        y = jnp.clip(there, 0, count - 1)
        fact = gathered_ref[y, start + corners : start + corners + 1, :].astype(jnp.int32)
        facts_ref[g : g + 1, :] = jnp.where((there >= 0) & (there < count), fact, 0)
        part = gathered_ref[y, start : start + corners, :]
        for s in range(slots):
            at = g * total + s * corners
            places_ref[at : at + corners, :] = jnp.broadcast_to(
                part[:, total + s : total + s + 1], (corners, LANES)
            )
    hots = hot_ref[...].astype(BF16)
    system = jnp.where(iota((n, 1), 0) == iota((1, n), 1), diag_ref[...], 0.0)
    for piece in thirds(spread_ref[...]):
        system = system + lax.dot_general(
            hots, piece.astype(BF16), (((0,), (0,)), ((), ())), preferred_element_type=F32
        )
    out_ref[...] = system
    eliminated(out_ref, 0, 2)


def rest_kernel(system_ref, out_ref):
    out_ref[...] = system_ref[...]
    eliminated(out_ref, 2, out_ref.shape[0] // LANES)


def eliminated(out_ref, first, last):
    n = out_ref.shape[0]
    b = LANES

    def eliminate(k, carry):
        ro = pl.multiple_of(k * b, b)
        pivots = split_inverse(out_ref[pl.ds(ro, b), pl.ds(ro, b)], b)
        col = out_ref[:, pl.ds(ro, b)]
        out_ref[:, pl.ds(ro, b)] = jnp.zeros((n, b), F32)
        out_ref[pl.ds(ro, b), pl.ds(ro, b)] = jnp.where(iota((b, b), 0) == iota((b, b), 1), 1.0, 0.0)
        fresh = high(pivots, out_ref[pl.ds(ro, b), :])
        out_ref[pl.ds(ro, b), :] = jnp.zeros((b, n), F32)
        at = iota((n, 1), 0)
        others = jnp.where((at >= ro) & (at < ro + b), 0.0, col)
        out_ref[...] = out_ref[...] - high(others, fresh)
        out_ref[pl.ds(ro, b), :] = fresh
        return carry

    lax.fori_loop(first, last, eliminate, 0)


def fact_of(facts, slots, corners, per, g, s, b, owned):
    k = facts[g, slots * corners + s * per + b]
    live = jnp.where(s < facts[g, slots * corners + slots * per], 1.0, 0.0)
    return k, jnp.where(k < owned, live, -live)


def gathered_rows(slots, corners, per, owned, g, facts, cand, u_ref):
    for s in range(slots):
        for b in range(per):
            k, sign = fact_of(facts, slots, corners, per, g, s, b, owned)
            row = cand[pl.ds(g * 5 * owned + k, 1), :] * sign
            u_ref[g * slots + s : g * slots + s + 1, b * LANES : (b + 1) * LANES] = row


def before_kernel(slots, corners, per, sweep, groups, parts, v_ref, last_ref, corner_ref, facts_ref, *rest):
    rest, (pay_ref, cand, u_ref, facts, sem) = rest[:-5], rest[-5:]
    packs, halo, extra = rest[:groups], rest[groups : groups + parts], rest[groups + parts :]
    copy = pltpu.make_async_copy(facts_ref, facts, sem)
    copy.start()
    owned = v_ref.shape[0]
    total = slots * corners
    v = v_ref[...]
    if groups > 1:
        cand[...] = jnp.zeros_like(cand)
        cand[9 * owned : 10 * owned, :] = v
        cand[13 * owned : 14 * owned, :] = v
    for i, ref in enumerate((v_ref, *halo)):
        cand[i * owned : (i + 1) * owned, :] = ref[...]
        if i < 3:
            pay_ref[i * owned : (i + 1) * owned, :] = ref[...]
    at = iota((owned, 1), 0)
    lane = iota((1, LANES), 1)
    energy = jnp.sum(v * v, keepdims=True)
    pays = []
    copy.wait()
    for g in range(groups):
        pack = packs[g]
        rows = (pack.shape[0] - 16) // slots
        pay = jnp.zeros((1, LANES), F32)
        gathered_rows(slots, corners, per, owned, g, facts, cand, u_ref)
        for s in range(slots):
            live = jnp.where(s < facts[g, total + slots * per], 1.0, 0.0)
            u = u_ref[g * slots + s : g * slots + s + 1, :]
            t = row_times(u, pack[s * rows : (s + 1) * rows, :].astype(BF16), 1)
            energy = energy + jnp.sum(t * t, keepdims=True)
            weights = pack[slots * rows + 8 + s : slots * rows + 9 + s, :]
            energy = energy + jnp.sum(weights * u * u, keepdims=True)
            first = s * corners
            if g:
                j = slots * rows
                narrow = [
                    pack[j : j + 8, i * LANES : (i + 1) * LANES] for i in range(total // 8)
                ]
                narrow = jnp.concatenate(narrow + [jnp.zeros((LANES - total, LANES), F32)], axis=0)
            else:
                narrow = corner_ref[...]
            c = row_times(t, narrow.astype(BF16), 1) * live
            pay = jnp.where((lane >= first) & (lane < first + corners), c, pay)
        pays.append(pay)
    cross = jnp.sum(v * last_ref[...], keepdims=True)
    pay = pays[0]
    if groups == 1:
        pay = jnp.where(lane == total + 2 * sweep, energy, pay)
    pay = jnp.where(lane == total + 2 * sweep + 1, cross, pay)
    for ref in extra:
        if ref.shape[0] == 1:
            pay = pay + ref[...]
        else:
            pay_ref[4 * owned :, :] = ref[...]
    block = jnp.where(at == 0, pay, 0.0)
    for g in range(1, groups):
        block = jnp.where(at == g, pays[g], block)
    pay_ref[3 * owned : 4 * owned, :] = block


def after_kernel(
    slots, corners, per, sweep, partial, y_ref, gathered_ref, rows_ref, places_ref, facts_ref, inverse_ref,
    *rest,
):
    packs, rest = rest[:3], rest[3:]
    before, rest = rest[: 1 if sweep else 0], rest[1 if sweep else 0 :]
    late, (cand, u_ref, acc, facts, sem) = rest[4:-5], rest[-5:]
    mine, east, west, sums_ref = rest[:4]
    copy = pltpu.make_async_copy(facts_ref, facts, sem)
    copy.start()
    owned = mine.shape[0]
    total = slots * corners
    n = inverse_ref.shape[0]
    count = gathered_ref.shape[0]
    middle = y_ref[0]
    field = {}
    for by in (0, 1, -1, 2, -2):
        y = middle + by
        inside = jnp.where((y >= 0) & (y < count), 1.0, 0.0)
        p = jnp.clip(y, 0, count - 1)
        for i in range(3 if abs(by) < 2 else 1):
            field[by, i] = gathered_ref[p, i * owned : (i + 1) * owned, :] * inside
    for g, by in enumerate((0, 1, -1)):
        parts = (field[by, 0], field[by, 1], field[by, 2])
        parts += (field[by + 1, 0] if by < 2 else None, field[by - 1, 0])
        for i, part in enumerate(parts):
            at = (5 * g + i) * owned
            cand[at : at + owned, :] = part
    lane = iota((1, LANES), 1)
    at = iota((n, 1), 0)
    spread = jnp.zeros((n, LANES), F32)
    totals = jnp.zeros((1, LANES), F32)
    places = rows_ref[...].astype(jnp.int32)
    for p in range(count):
        row = gathered_ref[p, 3 * owned : 3 * owned + 1, :]
        if partial and p > 0:
            row = row + gathered_ref[p - 1, 3 * owned + 1 : 3 * owned + 2, :]
        if partial and p < count - 1:
            row = row + gathered_ref[p + 1, 3 * owned + 2 : 3 * owned + 3, :]
        totals = totals + row
        spread = spread + jnp.where(places[p : p + 1, :] == at, row, 0.0)
    right = jnp.sum(jnp.where(lane < total, spread, 0.0), axis=1, keepdims=True)
    coarse = jnp.sum(inverse_ref[...] * right, axis=0, keepdims=True)
    wide = iota((1, n), 1)
    right_row = jnp.sum(jnp.where(at == wide, right, 0.0), axis=0, keepdims=True)
    energy = jnp.sum(coarse * right_row, keepdims=True)
    totals = totals + jnp.where(lane == total + 2 * sweep, energy, 0.0)
    for ref in before:
        totals = totals + ref[...]
    sums_ref[...] = totals
    acc[...] = jnp.zeros_like(acc)
    acc[:owned, :] = field[0, 0]
    copy.wait()
    for g in range(3):
        gathered_rows(slots, corners, per, owned, g, facts, cand, u_ref)
    wide = wide.astype(F32)
    local = jnp.sum(field[0, 0] * field[0, 0], keepdims=True)
    for g in range(3):
        pack = packs[g]
        rows = (pack.shape[0] - 16) // slots
        tail = slots * rows
        for s in range(slots):
            panel = pack[s * rows : (s + 1) * rows, :].astype(BF16)
            u = u_ref[g * slots + s : g * slots + s + 1, :]
            t = row_times(u, panel, 1)
            weights = pack[tail + 8 + s : tail + 9 + s, :]
            if g == 0:
                local = local + jnp.sum(t * t, keepdims=True)
                local = local + jnp.sum(weights * u * u, keepdims=True)
            for i in range(corners // 8):
                first = s * corners + 8 * i
                place = places_ref[g * total + first : g * total + first + 8, :1]
                back = jnp.sum(jnp.where(place == wide, coarse, 0.0), axis=1, keepdims=True)
                j = first // 8
                part = pack[tail : tail + 8, j * LANES : (j + 1) * LANES]
                t = t + jnp.sum(back * part, axis=0, keepdims=True)
            w = row_times(t, panel, 0) + weights * u
            for b in range(per):
                k, sign = fact_of(facts, slots, corners, per, g, s, b, owned)
                acc[pl.ds(g * 5 * owned + k, 1), :] += w[:, b * LANES : (b + 1) * LANES] * sign
    mine[...] = acc[:owned, :] + acc[9 * owned : 10 * owned, :] + acc[13 * owned : 14 * owned, :]
    for ref in late:
        ref[...] = jnp.where(lane == total + 2 * sweep, local, 0.0)
    east[...] = acc[owned : 2 * owned, :]
    west[...] = acc[2 * owned : 3 * owned, :]


def final_kernel(first, gathered_ref, rhs_ref, v0, v1, v2, w0, w1, mine, east, west, x_ref, r_ref):
    sums = gathered_ref[...]
    lane = iota((1, LANES), 1)

    def moment(i):
        return jnp.sum(jnp.where(lane == first + i, sums, 0.0), axis=1, keepdims=True)

    h00, r0, h11, h01, h22, h12 = (moment(i) for i in range(6))
    h02, r1, r2 = h11, STEP * h00, STEP * h01
    l10, l20 = h01 / h00, h02 / h00
    d1 = h11 - l10 * h01
    e12 = h12 - l10 * h02
    l21 = e12 / d1
    d2 = h22 - l20 * h02 - l21 * e12
    y1 = r1 - l10 * r0
    y2 = r2 - l20 * r0 - l21 * y1
    c2 = y2 / d2
    c1 = y1 / d1 - l21 * c2
    c0 = r0 / h00 - l10 * c1 - l20 * c2
    w2 = mine[...] + east[...] + west[...]
    x_ref[...] = c0 * v0[...] + c1 * v1[...] + c2 * v2[...]
    r_ref[...] = rhs_ref[...] - (c0 * w0[...] + c1 * w1[...] + c2 * w2)


def call(kernel, name, outs, scratch, scalars, arrays, space=pltpu.VMEM):
    vmem = pl.BlockSpec(memory_space=pltpu.VMEM)
    smem = pl.BlockSpec(memory_space=pltpu.SMEM)
    outs = [x if isinstance(x, jax.ShapeDtypeStruct) else jax.ShapeDtypeStruct(x, F32) for x in outs]
    return pl.pallas_call(
        kernel,
        out_shape=outs,
        in_specs=[smem] * len(scalars) + [pl.BlockSpec(memory_space=space)] * len(arrays),
        out_specs=[vmem] * len(outs),
        scratch_shapes=[pltpu.VMEM(x, F32) if isinstance(x, tuple) else x for x in scratch],
        compiler_params=pltpu.CompilerParams(vmem_limit_bytes=40 << 20),
        name=name,
    )(*scalars, *arrays)


def moved(x, axis, by):
    count = lax.axis_size(axis)
    return lax.ppermute(x, axis, [(i, i + by) for i in range(count) if 0 <= i + by < count])


def strided(count, by):
    return [list(range(i, count, by)) for i in range(by)]


def runs(count, size):
    return [list(range(i, i + size)) for i in range(0, count, size)]


def shards(
    panel, corner_panel, interface_diag, coarse_diag, scaling, dual_rhs, block_map, corner_map, counts
):
    slots, rows, width = panel.shape[2:]
    corners = corner_panel.shape[3]
    owned, block_size = scaling.shape[2:]
    n = coarse_diag.shape[1]
    total = slots * corners
    peers = lax.axis_size("gy")
    y = lax.axis_index("gy")
    per = block_map.shape[3]
    tile = (owned, block_size)
    facts_shape = jax.ShapeDtypeStruct((8, LANES), jnp.int32)
    facts_scratch = [pltpu.SMEM((8, LANES), jnp.int32), pltpu.SemaphoreType.DMA]
    rhs, scale = dual_rhs[0, 0], scaling[0, 0]
    direction = scale * rhs
    pack, report, corner_rows, facts = call(
        setup_kernel,
        "setup",
        [
            (slots * rows + 16, width),
            (corners + 8, LANES),
            (LANES, LANES),
            facts_shape,
        ],
        [
            pltpu.VMEM((slots, rows, width), BF16),
            pltpu.VMEM((slots, corners, rows), BF16),
            (slots, width),
            pltpu.VMEM((slots, corners), jnp.int32),
            pltpu.VMEM((slots, per), jnp.int32),
            pltpu.SMEM((1, 1), jnp.int32),
            (8, LANES),
            pltpu.SemaphoreType.DMA((6,)),
        ],
        [],
        [
            panel[0, 0],
            corner_panel[0, 0],
            interface_diag[0, 0],
            corner_map[0, 0],
            block_map[0, 0],
            counts,
        ],
        space=pltpu.HBM,
    )
    last = rhs
    directions, images, sums = [], [], []
    packs, late = [pack], []
    for sweep in range(3):
        partial = sweep == 1
        halo = [moved(direction, "gx", -1), moved(direction, "gx", 1)]
        if not partial:
            halo += [moved(direction, "gy", -1), moved(direction, "gy", 1)]
        extra = late if sweep else [report]
        size = 4 * owned + (0 if sweep else report.shape[0])
        groups = 3 if partial else 1
        (pay,) = call(
            functools.partial(before_kernel, slots, corners, per, sweep, groups, len(halo)),
            "before",
            [(size, LANES)],
            [(5 * groups * owned, block_size), (8, width), *facts_scratch],
            [],
            [
                direction,
                last,
                corner_rows,
                facts3 if partial else facts,
                *packs[:groups],
                *halo,
                *extra,
            ],
        )
        gathered = lax.all_gather(pay, "gy")
        if not sweep:
            here = y.reshape(1).astype(jnp.int32)
            started, place_rows, places3, facts3 = call(
                functools.partial(coarse_kernel, slots, corners, 4 * owned),
                "coarse",
                [(n, n), (peers, LANES), (3 * total, LANES), facts_shape],
                [(peers * total, n), (peers * total, n)],
                [here],
                [gathered, coarse_diag],
            )
            started, leaving = lax.optimization_barrier((started, pack))
            packs = [pack, moved(leaving, "gy", -1), moved(leaving, "gy", 1)]
            (inverse,) = call(rest_kernel, "rest", [(n, n)], [], [], [started])
        mine, east, west, sums, *late = call(
            functools.partial(after_kernel, slots, corners, per, sweep, partial),
            "after",
            [tile] * 3 + [(1, LANES)] * (2 if partial else 1),
            [(15 * owned, block_size), (8, width), (15 * owned, block_size), *facts_scratch],
            [here],
            [gathered, place_rows, places3, facts3, inverse, *packs, *([sums] if sweep else [])],
        )
        arrived = [moved(east, "gx", 1), moved(west, "gx", -1)]
        directions.append(direction)
        if sweep < 2:
            image = mine + arrived[0] + arrived[1]
            images.append(image)
            last, direction = image, STEP * scale * image
    across = lax.axis_size("gx")
    for group in (runs(across, 4), strided(across, 4)):
        sums = lax.all_gather(sums, "gx", axis=0, tiled=True, axis_index_groups=group)
        sums = jnp.sum(sums, axis=0, keepdims=True)
    multipliers, residual = call(
        functools.partial(final_kernel, total),
        "final",
        [tile] * 2,
        [],
        [],
        [sums, rhs, *directions, *images, mine, *arrived],
    )
    return multipliers[None, None], residual[None, None]


def solution(mesh):
    return jax.shard_map(
        shards,
        mesh=mesh,
        in_specs=(
            P("gx", "gy", None, None, None),
            P("gx", "gy", None, None, None),
            P("gx", "gy", None, None),
            P("gx", None),
            P("gx", "gy", None, None),
            P("gx", "gy", None, None),
            P("gx", "gy", None, None),
            P("gx", "gy", None, None),
            P("gx", "gy"),
        ),
        out_specs=(P("gx", "gy", None, None), P("gx", "gy", None, None)),
        check_vma=False,
    )
```
